128 devices in a mesh: section: 16 (over x, z), head: 8 (over y, core).
Axes of the slice: x: 4, y: 4, z: 4, core: 2. Of those that a mesh axis runs over, the one named last changes fastest.
Arguments:
- kv_cache: bfloat16 [2, 32, 2048, 576], P(None, 'section', 'head'), may hold values from -6 to 6
- prompt_len: int32 [32], replicated, may hold values from 1 to 2048, 32768 in all
- assign: int32 [32], replicated, may hold values from 0 to 31, each once
- row_slot: int32 [512], P('section'), may hold values from 0 to 1
- q_nope: bfloat16 [2, 2, 512, 16384], P(None, None, 'section', 'head'), may hold values from -6 to 6
- q_rope: bfloat16 [2, 2, 512, 8192], P(None, None, 'section', 'head'), may hold values from -500 to 500
- new_kv: bfloat16 [2, 2, 512, 576], P(None, None, 'section'), may hold values from -6 to 6
- w_uk: bfloat16 [2, 128, 128, 512], P(None, 'head'), may hold values from -0.5 to 0.5
- w_uv: bfloat16 [2, 128, 512, 128], P(None, 'head'), may hold values from -0.25 to 0.25
Outputs:
- head_out: bfloat16 [2, 2, 512, 16384], P(None, None, 'section', 'head')
The draws below stay inside these ranges and needn't reach their ends.
All inputs are finite; a program needn't handle non-finite values.
Results may differ from the reference program's by a relative error of at most 0.012.
Values may be sent and summed in bfloat16 or wider, within the bound.
No kernel may reach another device: no remote copies, remote signals or barrier semaphores. Data moves between devices by JAX's collectives and lax.ppermute only.
A program may use at most 128 MiB of HBM per device.

```python
import math
import jax
import jax.numpy as jnp
import numpy as np
from jax import lax

HEADS = 128
NOPE = 128
ROPE = 64
LAT = 512
VDIM = 128
LAYERS = 2
STEPS = 2
PPG = 2
LMAX = 2048
ROWS_DEV = 32
PROMPTS = 32
ROWS = 512
N_SECTION = 16


def draw_q_rope(key, part):
    key = jax.random.fold_in(key, 11)
    base = jnp.clip(jax.random.normal(key, (STEPS, LAYERS, ROWS, HEADS * ROPE), jnp.float32), -6.0, 6.0)
    return base.astype(jnp.bfloat16)


def with_ends(drawn, own_key, low, high):
    extent = drawn.shape
    spot = [jax.random.randint(jax.random.fold_in(own_key, axis), (), 0, extent[axis]) for axis in range(len(extent))]
    drawn = drawn.at[tuple(spot)].set(low)
    longest = extent.index(max(extent))
    spot[longest] = (spot[longest] + 1) % extent[longest]
    return drawn.at[tuple(spot)].set(high)


def block_scale(rng, shape, cuts, low, largest):
    def one(dim, parts):
        steps = jax.random.uniform(jax.random.fold_in(jax.random.fold_in(rng, 6), dim), (parts,), jnp.float32, low / len(cuts), largest / len(cuts))
        return jnp.repeat(jnp.exp(steps), shape[dim] // parts).reshape((-1,) + (1,) * (len(shape) - dim - 1))

    factor_of = one(*cuts[0])
    for cut in cuts[1:]:
        factor_of = factor_of * one(*cut)
    return factor_of


def split_up(amount, total, most, skew):
    weights = [(1 << 20) // math.isqrt(rank ** skew) + 1 for rank in range(2, amount + 1)]
    surplus, holding = total - most - (amount - 1), [1] * (amount - 1)
    while surplus > 0:
        movable = [i for i in range(amount - 1) if holding[i] < most]
        whole, left = sum([weights[i] for i in movable]), surplus
        for i in movable:
            addition = min(most - holding[i], max(1, left * weights[i] // whole), surplus)
            holding[i] = holding[i] + addition
            surplus = surplus - addition
    return np.array([most] + holding)


def uneven_parts(own_key, count, total, most, slope):
    if count == 2:
        one = jax.random.randint(own_key, (), max(1, total - most), min(most, total - 1) + 1)
        return jnp.stack([one, total - one])
    sizes = jnp.asarray(split_up(count, total, most, slope), jnp.int32)
    pairs = (count - 1) // 2
    source_of, taker = sizes[1:1 + 2 * pairs:2], sizes[2:2 + 2 * pairs:2]
    room = jnp.minimum(source_of - 1, most - taker)
    passed = jax.random.randint(jax.random.fold_in(own_key, 1), (pairs,), 0, 1 << 20) % (room + 1)
    sizes = sizes.at[1:1 + 2 * pairs:2].set(source_of - passed).at[2:2 + 2 * pairs:2].set(taker + passed)
    return sizes[jax.random.permutation(jax.random.fold_in(own_key, 2), count)]


def scatter_about(rng, shape, scale, reach, cuts=(), kind=jnp.bfloat16):
    values = scale * jax.random.normal(rng, shape, jnp.float32)
    if cuts:
        values = values * block_scale(rng, shape, cuts, -0.22, 0.18)
    return jnp.clip(values, -reach, reach).astype(kind)


def setup_inputs(seed: int = 0) -> dict:
    arg_keys = jax.random.split(jax.random.key(seed), 10)
    return {
        "kv_cache": scatter_about(arg_keys[0], (LAYERS, PROMPTS, LMAX, LAT + ROPE), 1.0, 6.0, ((1, 16), (2, 8))),
        "prompt_len": uneven_parts(arg_keys[1], PROMPTS, PROMPTS * LMAX // 2, LMAX, 2).astype(jnp.int32),
        "assign": jax.random.permutation(arg_keys[2], PROMPTS).astype(jnp.int32),
        "row_slot": with_ends(jax.random.randint(arg_keys[3], (ROWS,), 0, PPG), jax.random.fold_in(arg_keys[3], 1), 0, PPG - 1).astype(jnp.int32),
        "q_nope": scatter_about(arg_keys[4], (STEPS, LAYERS, ROWS, HEADS * NOPE), 1.0, 6.0, ((2, 16), (3, 8))),
        "q_rope": draw_q_rope(jax.random.fold_in(arg_keys[9], 71), 0),
        "new_kv": scatter_about(arg_keys[6], (STEPS, LAYERS, ROWS, LAT + ROPE), 1.0, 6.0, ((2, 16),)),
        "w_uk": scatter_about(arg_keys[7], (LAYERS, HEADS, NOPE, LAT), NOPE ** -0.5, 0.5, ((1, 8),)),
        "w_uv": scatter_about(arg_keys[8], (LAYERS, HEADS, LAT, VDIM), LAT ** -0.5, 0.25, ((1, 8),)),
    }


def attend(query, cache, new_keys, slots, lengths):
    keys_flat = cache.reshape(PPG * LMAX, LAT + ROPE).astype(jnp.float32)
    scale = (NOPE + ROPE) ** -0.5
    scores = jnp.einsum('rhc,kc->rhk', query.astype(jnp.float32), keys_flat) * scale
    own = jnp.einsum('rhc,trc->rht', query.astype(jnp.float32), new_keys.astype(jnp.float32)) * scale
    index = jnp.arange(PPG * LMAX, dtype=jnp.int32)
    slot_of = index // LMAX
    position = index % LMAX
    valid = (slot_of[None, :] == slots[:, None]) & (position[None, :] < lengths[slot_of][None, :])
    scores = jnp.where(valid[:, None, :], scores, -jnp.inf)
    top = jnp.maximum(jnp.max(scores, axis=2), jnp.max(own, axis=2))
    exp_keys = jnp.exp(scores - top[:, :, None])
    exp_own = jnp.exp(own - top[:, :, None])
    total = jnp.sum(exp_keys, axis=2) + jnp.sum(exp_own, axis=2)
    weight_keys = exp_keys.astype(jnp.bfloat16).astype(jnp.float32)
    weight_own = exp_own.astype(jnp.bfloat16).astype(jnp.float32)
    summed = jnp.einsum('rhk,kc->rhc', weight_keys, keys_flat[:, :LAT])
    summed = summed + jnp.einsum('rht,trc->rhc', weight_own, new_keys[:, :, :LAT].astype(jnp.float32))
    return (summed / total[:, :, None]).astype(jnp.bfloat16)


def reference(kv_cache, prompt_len, assign, row_slot, q_nope, q_rope, new_kv, w_uk, w_uv):
    outputs = []
    for step in range(STEPS):
        per_layer = []
        for layer in range(LAYERS):
            nope = q_nope[step, layer].reshape(ROWS, HEADS, NOPE).astype(jnp.float32)
            q_lat = jnp.einsum('rhn,hnc->rhc', nope, w_uk[layer].astype(jnp.float32)).astype(jnp.bfloat16)
            query = jnp.concatenate([q_lat, q_rope[step, layer].reshape(ROWS, HEADS, ROPE)], axis=2)

            def one_group(group):
                chosen = lax.dynamic_slice(assign, (group * PPG,), (PPG,))
                cache = kv_cache[layer][chosen]
                lengths = prompt_len[chosen]
                start = (group * ROWS_DEV).astype(jnp.int32)
                rows_q = lax.dynamic_slice_in_dim(query, start, ROWS_DEV, 0)
                slots = lax.dynamic_slice_in_dim(row_slot, start, ROWS_DEV, 0)
                new_keys = lax.dynamic_slice_in_dim(new_kv[:step + 1, layer], start, ROWS_DEV, 1)
                o_lat = attend(rows_q, cache, new_keys, slots, lengths)
                result = jnp.einsum('rhc,hcv->rhv', o_lat.astype(jnp.float32), w_uv[layer].astype(jnp.float32))
                return result.astype(jnp.bfloat16)

            groups = lax.map(one_group, jnp.arange(N_SECTION, dtype=jnp.int32))
            per_layer.append(groups.reshape(ROWS, HEADS * VDIM))
        outputs.append(jnp.stack(per_layer))
    return jnp.stack(outputs)
```

```python
import functools
import math

import jax
import jax.numpy as jnp
from jax import lax
from jax.experimental import pallas as pl
from jax.experimental.pallas import tpu as pltpu
from jax.sharding import PartitionSpec as P

BF = jnp.bfloat16
F32 = jnp.float32
TILE_ROWS = 8
LOW = -1e30
MIB = 1 << 20


def params(limit, **extra):
    return pltpu.CompilerParams(vmem_limit_bytes=limit * MIB, **extra)


def cost(flops, nbytes, trans=0):
    return pl.CostEstimate(flops=int(flops), bytes_accessed=int(nbytes), transcendentals=int(trans))


def pack_body(lat, kv_ref, x0_ref, x1_ref):
    parts = x0_ref.shape[0]
    rows = x0_ref.shape[2]
    a = kv_ref[0, 0]
    b = kv_ref[1, 0]
    x0 = jnp.concatenate([a[:, :lat], a[:, lat:], b[:, lat:]], axis=1)
    x0_ref[:, 0] = x0.reshape(parts, rows, x0.shape[1])
    x1_ref[:, 0] = b[:, :lat].reshape(parts, rows, lat)


def pack(kv, parts, lat):
    layers, prompts, tok, width = kv.shape
    wide = lat + 2 * (width - lat)
    rows = tok // parts
    return pl.pallas_call(
        functools.partial(pack_body, lat),
        grid=(prompts,),
        in_specs=[pl.BlockSpec((layers, 1, tok, width), lambda p: (0, p, 0, 0))],
        out_specs=[
            pl.BlockSpec((parts, 1, rows, wide), lambda p: (0, p, 0, 0)),
            pl.BlockSpec((parts, 1, rows, lat), lambda p: (0, p, 0, 0)),
        ],
        out_shape=[
            jax.ShapeDtypeStruct((parts, prompts, rows, wide), BF),
            jax.ShapeDtypeStruct((parts, prompts, rows, lat), BF),
        ],
        compiler_params=params(16),
        cost_estimate=cost(0, 2 * kv.size * 2),
        name="pack",
    )(kv)


def pick_body(assign_ref, x_ref, o_ref):
    for i in range(o_ref.shape[0]):
        o_ref[i] = x_ref[assign_ref[i]]


def pick(assign, x):
    flat = x.reshape((-1,) + x.shape[2:])
    out = pl.pallas_call(
        pick_body,
        in_specs=[
            pl.BlockSpec(memory_space=pltpu.SMEM),
            pl.BlockSpec(memory_space=pltpu.VMEM),
        ],
        out_specs=pl.BlockSpec(memory_space=pltpu.VMEM),
        out_shape=jax.ShapeDtypeStruct(flat.shape, BF),
        compiler_params=params(16),
        cost_estimate=cost(0, 2 * x.size * 2),
        name="pick",
    )(assign, flat)
    return out.reshape(x.shape)


def row_places(slot_ref):
    n = slot_ref.shape[0]
    ones = jnp.int32(0)
    for r in range(n):
        ones = ones + slot_ref[r]
    zeros = n - ones
    tiles0 = lax.div(zeros + (TILE_ROWS - 1), jnp.int32(TILE_ROWS))
    tiles1 = lax.div(ones + (TILE_ROWS - 1), jnp.int32(TILE_ROWS))
    places = []
    c0, c1 = jnp.int32(0), tiles0 * TILE_ROWS
    for r in range(n):
        s = slot_ref[r]
        places.append(jnp.where(s == 0, c0, c1))
        c0 = c0 + (1 - s)
        c1 = c1 + s
    return places, tiles0, tiles1


def order_index(axis, shape, steps):
    i = lax.broadcasted_iota(jnp.int32, shape, axis)
    per = TILE_ROWS * steps
    tile = i // per
    rest = i - tile * per
    step = rest // TILE_ROWS
    return tile * TILE_ROWS + (rest - step * TILE_ROWS), step


def split3(x):
    hi = x.astype(BF).astype(F32)
    mid = (x - hi).astype(BF).astype(F32)
    lo = x - hi - mid
    return hi, mid, lo


def with_lse(o, lse):
    hi, mid, lo = split3(lse)
    lane = lax.broadcasted_iota(jnp.int32, (o.shape[0], 128), 1)
    tail = jnp.where(lane == 0, hi, jnp.where(lane == 1, mid, jnp.where(lane == 2, lo, 0.0)))
    return jnp.concatenate([o.astype(BF), tail.astype(BF)], axis=1)


def query_body(layer, steps, scale, slot_ref, nope_ref, rope_ref, w_ref, nk_ref, q_ref, n_ref, perm_ref, own_ref):
    tiles, heads, per, wide = q_ref.shape
    rows = nope_ref.shape[2]
    nope = w_ref.shape[2]
    lat = w_ref.shape[3]
    total = tiles * per

    @pl.when(pl.program_id(0) == 0)
    def _():
        places, _, _ = row_places(slot_ref)
        lane = lax.broadcasted_iota(jnp.int32, (1, steps * rows), 1)
        step_of = lane // rows
        row_of = lane - step_of * rows
        where_to = jnp.full((1, steps * rows), -1, jnp.int32)
        for r in range(rows):
            where_to = jnp.where(row_of == r, places[r], where_to)
        place, step = order_index(0, (total, steps * rows), steps)
        perm_ref[...] = jnp.where((place == where_to) & (step == step_of), 1.0, 0.0).astype(BF)
        lane1 = lax.broadcasted_iota(jnp.int32, (total, rows), 1)
        place1, _ = order_index(0, (total, rows), steps)
        where1 = jnp.full((1, rows), -1, jnp.int32)
        lane_r = lax.broadcasted_iota(jnp.int32, (1, rows), 1)
        for r in range(rows):
            where1 = jnp.where(lane_r == r, places[r], where1)
        by_row = jnp.where(place1 == where1, 1.0, 0.0).astype(BF)
        for s in range(steps):
            own_ref[s] = jnp.dot(by_row, nk_ref[s, 0], preferred_element_type=F32)

    perm = perm_ref[...]
    x = nope_ref[:, 0].reshape(steps * rows, heads * nope)
    x = jnp.dot(perm, x, preferred_element_type=F32).astype(BF)
    r = rope_ref[:, 0].reshape(steps * rows, 128)
    r = jnp.dot(perm, r, preferred_element_type=F32)
    rolled = pltpu.roll(r, 64, 1)
    lane = lax.broadcasted_iota(jnp.int32, (total, 128), 1)
    mine = (lane // 64) == layer
    _, step = order_index(0, (total, 1), steps)
    for h in range(heads):
        ql = jnp.dot(x[:, h * nope:(h + 1) * nope], w_ref[0, h], preferred_element_type=F32).astype(BF)
        qr = jnp.where(mine, r if h == layer else rolled, 0.0).astype(BF)
        q = jnp.concatenate([ql, qr], axis=1)
        q_ref[:, h] = q.reshape(tiles, per, wide)
        qf = q.astype(F32)
        scores = []
        for s in range(steps):
            v = jnp.sum(qf * own_ref[s], axis=1, keepdims=True) * scale
            scores.append(jnp.where(step >= s, v, LOW))
        top = functools.reduce(jnp.maximum, scores)
        weights = [jnp.exp(v - top) for v in scores]
        all_w = functools.reduce(lambda a, b: a + b, weights)
        o = weights[0] * own_ref[0, :, :lat]
        for s in range(1, steps):
            o = o + weights[s] * own_ref[s, :, :lat]
        n_ref[:, h] = with_lse(o / all_w, top + jnp.log(all_w)).reshape(tiles, per, wide)


def queries(layer, tiles, scale, row_slot, q_nope, q_rope, w_uk, nk):
    steps, _, rows, _ = q_nope.shape
    _, heads, nope, lat = w_uk.shape
    wide = nk.shape[3]
    per = TILE_ROWS * steps
    shape = jax.ShapeDtypeStruct((tiles, heads, per, wide), BF)
    return pl.pallas_call(
        functools.partial(query_body, layer, steps, scale),
        grid=(heads // 2,),
        in_specs=[
            pl.BlockSpec(memory_space=pltpu.SMEM),
            pl.BlockSpec((steps, 1, rows, 2 * nope), lambda h: (0, layer, 0, h)),
            pl.BlockSpec((steps, 1, rows, 128), lambda h: (0, layer, 0, h)),
            pl.BlockSpec((1, 2, nope, lat), lambda h: (layer, h, 0, 0)),
            pl.BlockSpec((steps, 1, rows, wide), lambda h: (0, layer, 0, 0)),
        ],
        out_specs=[pl.BlockSpec((tiles, 2, per, wide), lambda h: (0, h, 0, 0))] * 2,
        out_shape=[shape, shape],
        scratch_shapes=[
            pltpu.VMEM((tiles * per, steps * rows), BF),
            pltpu.VMEM((steps, tiles * per, wide), F32),
        ],
        compiler_params=params(16),
        cost_estimate=cost(2 * tiles * per * heads * nope * lat, w_uk.size + 4 * tiles * per * heads * wide),
        name="queries",
    )(row_slot, q_nope, q_rope, w_uk, nk)


def attend_body(layer, scale, slot_ref, assign_ref, len_ref, qa_ref, qb_ref, *refs):
    pieces = refs[:4]
    ropes = refs[4:8] if layer else None
    oa_ref, ob_ref, keys, sems = refs[-4:]
    per_group = 2
    group = lax.axis_index("section")
    head = lax.axis_index("head")
    y = lax.div(head, jnp.int32(2))
    core = lax.rem(head, jnp.int32(2))
    tile = pl.program_id(0)
    wide = keys.shape[-1]
    lat = oa_ref.shape[3] - 128
    block = keys.shape[2] * keys.shape[3]
    _, heads, per, _ = qa_ref.shape
    count = heads * per

    @pl.when(tile == 0)
    def _():
        copies = []
        for k in range(4):
            at = lax.rem(y - k + 4, jnp.int32(4))
            for s in range(per_group):
                if layer == 0:
                    copies.append(pltpu.make_async_copy(pieces[k].at[:, s], keys.at[s, at], sems.at[k, s, 0]))
                else:
                    copies.append(pltpu.make_async_copy(
                        pieces[k].at[:, s], keys.at[s, at, :, :, pl.ds(0, lat)], sems.at[k, s, 0]))
                    copies.append(pltpu.make_async_copy(
                        ropes[k].at[:, s, :, pl.ds(lat, 128)], keys.at[s, at, :, :, pl.ds(lat, 128)], sems.at[k, s, 1]))
        for c in copies:
            c.start()
        for c in copies:
            c.wait()

    zeros = jnp.int32(slot_ref.shape[0])
    for r in range(slot_ref.shape[0]):
        zeros = zeros - slot_ref[r]
    tiles0 = lax.div(zeros + (TILE_ROWS - 1), jnp.int32(TILE_ROWS))
    tiles1 = lax.div(slot_ref.shape[0] - zeros + (TILE_ROWS - 1), jnp.int32(TILE_ROWS))
    slot = jnp.where(tile < tiles0, 0, 1)
    length = len_ref[assign_ref[group * per_group + slot]]
    blocks = lax.div(length - block * core + (2 * block - 1), jnp.int32(2 * block))
    blocks = jnp.where(tile < tiles0 + tiles1, jnp.clip(blocks, 0, 4), 0)
    factor = scale * math.log2(math.e)

    @pl.when(blocks == 0)
    def _():
        nothing = with_lse(jnp.zeros((count, lat), F32), jnp.full((count, 1), LOW, F32)).reshape(heads, per, wide)
        oa_ref[0] = nothing
        ob_ref[0] = nothing

    for n in range(1, 5):
        @pl.when(blocks == n)
        def _(n=n):
            left = length - (2 * (n - 1) + core) * block
            k = keys[slot, 0:n].reshape(n * block, wide)
            lane = lax.broadcasted_iota(jnp.int32, (count, block), 1)
            for q_ref, o_ref in ((qa_ref, oa_ref), (qb_ref, ob_ref)):
                q = q_ref[0].reshape(count, wide)
                s = lax.dot_general(q, k, (((1,), (1,)), ((), ())), preferred_element_type=F32)
                last = jnp.where(lane < left, s[:, (n - 1) * block:], LOW)
                s = last if n == 1 else jnp.concatenate([s[:, :(n - 1) * block], last], axis=1)
                top = jnp.max(s, axis=1, keepdims=True)
                p = jnp.exp2((s - top) * factor)
                total = jnp.sum(p, axis=1, keepdims=True)
                o = jnp.dot(p.astype(BF), k[:, :lat], preferred_element_type=F32)
                o_ref[0] = with_lse(o / total, top * scale + jnp.log(total)).reshape(heads, per, wide)


def attend(layer, scale, row_slot, assign, prompt_len, qa, qb, pieces, ropes):
    tiles, heads, per, wide = qa.shape
    parts, slots, rows, _ = pieces[0].shape
    spec = pl.BlockSpec((1, heads, per, wide), lambda i: (i, 0, 0, 0))
    smem = pl.BlockSpec(memory_space=pltpu.SMEM)
    held = list(pieces) + (list(ropes) if layer else [])
    shape = jax.ShapeDtypeStruct(qa.shape, BF)
    return pl.pallas_call(
        functools.partial(attend_body, layer, scale),
        grid=(tiles,),
        in_specs=[smem] * 3 + [spec] * 2 + [pl.BlockSpec(memory_space=pl.ANY)] * len(held),
        out_specs=[spec] * 2,
        out_shape=[shape, shape],
        scratch_shapes=[
            pltpu.VMEM((slots, 4, parts, rows, wide), BF),
            pltpu.SemaphoreType.DMA((4, slots, 2)),
        ],
        compiler_params=params(32),
        cost_estimate=cost(2 * 2 * tiles * heads * per * 4 * parts * rows * 1152, 4 * qa.size * 2, 0),
        name="attend",
    )(row_slot, assign, prompt_len, qa, qb, *held)


def merge_body(layer, steps, slot_ref, a_ref, b_ref, c_ref, w_ref, *refs):
    o_ref, back_ref = refs[-2:]
    tiles, heads, per, wide = a_ref.shape
    lat = wide - 128
    total = tiles * per
    rows = o_ref.shape[2]

    @pl.when(pl.program_id(0) == 0)
    def _():
        places, _, _ = row_places(slot_ref)
        sub = lax.broadcasted_iota(jnp.int32, (steps * rows, total), 0)
        step_of = sub // rows
        row_of = sub - step_of * rows
        where_to = jnp.full((steps * rows, total), -1, jnp.int32)
        for r in range(rows):
            where_to = jnp.where(row_of == r, places[r], where_to)
        place, step = order_index(1, (steps * rows, total), steps)
        back_ref[...] = jnp.where((place == where_to) & (step == step_of), 1.0, 0.0).astype(BF)

    back = back_ref[...]
    for h in range(heads):
        parts = [r[:, h].reshape(total, wide) for r in (a_ref, b_ref, c_ref)]
        lse = [jnp.sum(p[:, lat:].astype(F32), axis=1, keepdims=True) for p in parts]
        top = functools.reduce(jnp.maximum, lse)
        w = [jnp.exp(v - top) for v in lse]
        inv = 1.0 / (w[0] + w[1] + w[2])
        o = sum((wi * inv) * p[:, :lat].astype(F32) for wi, p in zip(w, parts))
        res = jnp.dot(o.astype(BF), w_ref[0, h], preferred_element_type=F32).astype(BF)
        res = jnp.dot(back, res, preferred_element_type=F32).astype(BF)
        value = res.shape[1]
        o_ref[:, 0, :, h * value:(h + 1) * value] = res.reshape(steps, rows, value)


def merge(layer, layers, steps, rows, row_slot, a, b, c, w_uv, before):
    tiles, heads, per, wide = a.shape
    lat, value = w_uv.shape[2:]
    spec = pl.BlockSpec((tiles, 2, per, wide), lambda h: (0, h, 0, 0))
    held = [] if before is None else [before]
    return pl.pallas_call(
        functools.partial(merge_body, layer, steps),
        grid=(heads // 2,),
        in_specs=[pl.BlockSpec(memory_space=pltpu.SMEM)] + [spec] * 3
        + [pl.BlockSpec((1, 2, lat, value), lambda h: (layer, h, 0, 0))]
        + [pl.BlockSpec(memory_space=pl.ANY)] * len(held),
        out_specs=pl.BlockSpec((steps, 1, rows, 2 * value), lambda h: (0, layer, 0, h)),
        out_shape=jax.ShapeDtypeStruct((steps, layers, rows, heads * value), BF),
        scratch_shapes=[pltpu.VMEM((steps * rows, tiles * per), BF)],
        input_output_aliases={5: 0} if held else {},
        compiler_params=params(16),
        cost_estimate=cost(2 * tiles * per * heads * lat * value, 3 * a.size * 2),
        name="merge",
    )(row_slot, a, b, c, w_uv, *held)


def local(n_section, n_head, kv_cache, prompt_len, assign, row_slot, q_nope, q_rope, new_kv, w_uk, w_uv):
    layers = kv_cache.shape[0]
    steps, _, rows, _ = q_nope.shape
    _, heads, nope, lat = w_uk.shape
    width = kv_cache.shape[3]
    rope = width - lat
    scale = (nope + rope) ** (-0.5)
    tiles = rows // TILE_ROWS + 1
    chips = n_head // 2

    def spread(x):
        return lax.all_to_all(x, "section", 0, 0, tiled=True)

    def along_y(x):
        out = [x]
        for k in range(1, chips):
            out.append(lax.ppermute(x, "head", [(h, ((h // 2 + k) % chips) * 2 + h % 2) for h in range(n_head)]))
        return out

    def swap(x):
        return lax.ppermute(x, "head", [(h, h ^ 1) for h in range(n_head)])

    x0, x1 = pack(kv_cache, n_section, lat)
    k0 = spread(pick(assign, spread(x0)))
    k1 = spread(pick(assign, spread(x1)))

    zero = jnp.zeros((steps, rows, rope), BF)
    nk = jnp.stack([
        jnp.concatenate([new_kv[:, 0], zero], axis=2),
        jnp.concatenate([new_kv[:, 1, :, :lat], zero, new_kv[:, 1, :, lat:]], axis=2),
    ], axis=1)
    qn = [queries(layer, tiles, scale, row_slot, q_nope, q_rope, w_uk, nk) for layer in range(layers)]
    sib = [swap(q) for q, _ in qn]

    p0 = along_y(k0)
    p1 = along_y(k1)
    out = None
    for layer, pieces in enumerate((p0, p1)):
        mine, theirs = attend(layer, scale, row_slot, assign, prompt_len, qn[layer][0], sib[layer], pieces, p0)
        out = merge(layer, layers, steps, rows, row_slot, mine, swap(theirs), qn[layer][1], w_uv, out)
    return out


def solution(mesh):
    in_specs = (
        P(None, "section", "head", None),
        P(),
        P(),
        P("section"),
        P(None, None, "section", "head"),
        P(None, None, "section", "head"),
        P(None, None, "section", None),
        P(None, "head", None, None),
        P(None, "head", None, None),
    )
    out_specs = P(None, None, "section", "head")
    step = functools.partial(local, mesh.shape["section"], mesh.shape["head"])
    return jax.shard_map(step, mesh=mesh, in_specs=in_specs, out_specs=out_specs, check_vma=False)
```

```python
import functools
import math

import jax
import jax.numpy as jnp
from jax import lax
from jax.experimental import pallas as pl
from jax.experimental.pallas import tpu as pltpu
from jax.sharding import PartitionSpec as P

BF = jnp.bfloat16
F32 = jnp.float32
TILE_ROWS = 8
LOW = -1e30
MIB = 1 << 20


def params(limit, **extra):
    return pltpu.CompilerParams(vmem_limit_bytes=limit * MIB, **extra)


def cost(flops, nbytes, trans=0):
    return pl.CostEstimate(flops=int(flops), bytes_accessed=int(nbytes), transcendentals=int(trans))


def pack_body(lat, kv_ref, x_ref):
    parts, _, rows, wide = x_ref.shape
    a = kv_ref[0, 0].T
    b = kv_ref[1, 0].T
    x = jnp.concatenate([a[:, :lat], b[:, :lat], a[:, lat:], b[:, lat:]], axis=1)
    x_ref[:, 0] = x.reshape(parts, rows, wide)


def pack(kv, parts, lat):
    layers, prompts, tok, width = kv.shape
    rows = tok // parts
    return pl.pallas_call(
        functools.partial(pack_body, lat),
        grid=(prompts,),
        in_specs=[pl.BlockSpec((layers, 1, width, tok), lambda p: (0, p, 0, 0))],
        out_specs=pl.BlockSpec((parts, 1, rows, layers * width), lambda p: (0, p, 0, 0)),
        out_shape=jax.ShapeDtypeStruct((parts, prompts, rows, layers * width), BF),
        compiler_params=params(16),
        cost_estimate=cost(0, 2 * kv.size * 2),
        name="pack",
    )(kv.transpose(0, 1, 3, 2))


def pick_body(layer, lat, assign_ref, x_ref, o_ref):
    for i in range(o_ref.shape[0]):
        p = assign_ref[i]
        o_ref[i, :, :lat] = x_ref[p, :, layer * lat:(layer + 1) * lat]
        if layer == 0:
            o_ref[i, :, lat:] = x_ref[p, :, 2 * lat:]


def pick(layer, lat, assign, x):
    groups, slots, rows, wide = x.shape
    out = lat if layer else wide - lat
    res = pl.pallas_call(
        functools.partial(pick_body, layer, lat),
        in_specs=[
            pl.BlockSpec(memory_space=pltpu.SMEM),
            pl.BlockSpec(memory_space=pltpu.VMEM),
        ],
        out_specs=pl.BlockSpec(memory_space=pltpu.VMEM),
        out_shape=jax.ShapeDtypeStruct((groups * slots, rows, out), BF),
        compiler_params=params(16),
        cost_estimate=cost(0, 2 * x.size * 2),
        name="pick",
    )(assign, x.reshape(groups * slots, rows, wide))
    return res.reshape(groups, slots, rows, out)


def count_zeros(slot_ref):
    zeros = jnp.int32(slot_ref.shape[0])
    for r in range(slot_ref.shape[0]):
        zeros = zeros - slot_ref[r]
    return zeros


def row_places(slot_ref):
    places = []
    c0, c1 = jnp.int32(0), count_zeros(slot_ref)
    for r in range(slot_ref.shape[0]):
        s = slot_ref[r]
        places.append(jnp.where(s == 0, c0, c1))
        c0 = c0 + (1 - s)
        c1 = c1 + s
    return places


def order_index(axis, shape, steps):
    i = lax.broadcasted_iota(jnp.int32, shape, axis)
    per = TILE_ROWS * steps
    tile = i // per
    rest = i - tile * per
    step = rest // TILE_ROWS
    return tile * TILE_ROWS + (rest - step * TILE_ROWS), step


def split2(x):
    hi = x.astype(BF).astype(F32)
    return hi, (x - hi).astype(BF).astype(F32)


def partial_of(o, top, total):
    lane = lax.broadcasted_iota(jnp.int32, (o.shape[0], 128), 1)
    tail = jnp.zeros((o.shape[0], 128), F32)
    for i, v in enumerate(top + total):
        tail = jnp.where(lane == i, v, tail)
    return jnp.concatenate([o, tail], axis=1)


def query_body(layer, steps, scale, slot_ref, nope_ref, rope_ref, w_ref, nk_ref, q_ref, n_ref, perm_ref, own_ref):
    tiles, heads, per, wide = q_ref.shape
    rows = nope_ref.shape[2]
    nope = w_ref.shape[2]
    lat = w_ref.shape[3]
    total = tiles * per

    @pl.when(pl.program_id(0) == 0)
    def _():
        places = row_places(slot_ref)
        lane = lax.broadcasted_iota(jnp.int32, (1, steps * rows), 1)
        step_of = lane // rows
        row_of = lane - step_of * rows
        where_to = jnp.full((1, steps * rows), -1, jnp.int32)
        for r in range(rows):
            where_to = jnp.where(row_of == r, places[r], where_to)
        place, step = order_index(0, (total, steps * rows), steps)
        perm_ref[...] = jnp.where((place == where_to) & (step == step_of), 1.0, 0.0).astype(BF)
        lane1 = lax.broadcasted_iota(jnp.int32, (total, rows), 1)
        place1, _ = order_index(0, (total, rows), steps)
        where1 = jnp.full((1, rows), -1, jnp.int32)
        lane_r = lax.broadcasted_iota(jnp.int32, (1, rows), 1)
        for r in range(rows):
            where1 = jnp.where(lane_r == r, places[r], where1)
        by_row = jnp.where(place1 == where1, 1.0, 0.0).astype(BF)
        for s in range(steps):
            own_ref[s] = jnp.dot(by_row, nk_ref[s, 0], preferred_element_type=F32)

    perm = perm_ref[...]
    x = nope_ref[:, 0].reshape(steps * rows, heads * nope)
    x = jnp.dot(perm, x, preferred_element_type=F32).astype(BF)
    r = rope_ref[:, 0].reshape(steps * rows, 128)
    r = jnp.dot(perm, r, preferred_element_type=F32)
    rolled = pltpu.roll(r, 64, 1)
    lane = lax.broadcasted_iota(jnp.int32, (total, 128), 1)
    mine = (lane // 64) == layer
    _, step = order_index(0, (total, 1), steps)
    for h in range(heads):
        ql = jnp.dot(x[:, h * nope:(h + 1) * nope], w_ref[0, h], preferred_element_type=F32).astype(BF)
        qr = jnp.where(mine, r if h == layer else rolled, 0.0).astype(BF)
        q = jnp.concatenate([ql, qr], axis=1)
        q_ref[:, h] = q.reshape(tiles, per, wide)
        qf = q.astype(F32)
        scores = []
        for s in range(steps):
            v = jnp.sum(qf * own_ref[s], axis=1, keepdims=True) * scale
            scores.append(jnp.where(step >= s, v, LOW))
        top = split2(functools.reduce(jnp.maximum, scores))
        weights = [jnp.exp(v - (top[0] + top[1])) for v in scores]
        o = weights[0] * own_ref[0, :, :lat]
        for s in range(1, steps):
            o = o + weights[s] * own_ref[s, :, :lat]
        part = partial_of(o, top, split2(sum(weights)))
        n_ref[:, h] = part.astype(BF).reshape(tiles, per, wide)


def queries(layer, tiles, scale, row_slot, q_nope, q_rope, w_uk, nk):
    steps, _, rows, _ = q_nope.shape
    _, heads, nope, lat = w_uk.shape
    wide = nk.shape[3]
    per = TILE_ROWS * steps
    shape = jax.ShapeDtypeStruct((tiles, heads, per, wide), BF)
    return pl.pallas_call(
        functools.partial(query_body, layer, steps, scale),
        grid=(heads // 2,),
        in_specs=[
            pl.BlockSpec(memory_space=pltpu.SMEM),
            pl.BlockSpec((steps, 1, rows, 2 * nope), lambda h: (0, layer, 0, h)),
            pl.BlockSpec((steps, 1, rows, 128), lambda h: (0, layer, 0, h)),
            pl.BlockSpec((1, 2, nope, lat), lambda h: (layer, h, 0, 0)),
            pl.BlockSpec((steps, 1, rows, wide), lambda h: (0, layer, 0, 0)),
        ],
        out_specs=[pl.BlockSpec((tiles, 2, per, wide), lambda h: (0, h, 0, 0))] * 2,
        out_shape=[shape, shape],
        scratch_shapes=[
            pltpu.VMEM((tiles * per, steps * rows), BF),
            pltpu.VMEM((steps, tiles * per, wide), F32),
        ],
        compiler_params=params(16),
        cost_estimate=cost(2 * tiles * per * heads * nope * lat, w_uk.size + 4 * tiles * per * heads * wide),
        name="queries",
    )(row_slot, q_nope, q_rope, w_uk, nk)


def attend_body(layer, scale, shifts, slot_ref, assign_ref, len_ref, qa_ref, qb_ref, *refs):
    names = [(k, i) for k in shifts for i in range(2 if k == 2 else 1)]
    pieces = refs[:len(names)]
    ropes = refs[len(names):2 * len(names)] if layer else None
    oa_ref, ob_ref, keys, sems = refs[-4:]
    slots = keys.shape[0]
    group = lax.axis_index("section")
    head = lax.axis_index("head")
    y = lax.div(head, jnp.int32(2))
    core = lax.rem(head, jnp.int32(2))
    wide = keys.shape[-1]
    lat = wide - 128
    block = keys.shape[2] * keys.shape[3]
    tiles, heads, per, _ = qa_ref.shape
    count = heads * per
    half = keys.shape[2] // 2
    own = lat if layer else wide
    origin = {k: lax.rem(y - k + 4, jnp.int32(4)) for k in shifts}

    def copies(s):
        out = []
        for j, (k, i) in enumerate(names):
            at = sum(jnp.where(origin[o] < origin[k], 1, 0) for o in shifts)
            to = pl.ds(i * half, half) if k == 2 else pl.ds(0, 2 * half)
            out.append(pltpu.make_async_copy(
                pieces[j].at[:, s], keys.at[s, at, to, :, pl.ds(0, own)], sems.at[k, s, i]))
            if layer:
                out.append(pltpu.make_async_copy(
                    ropes[j].at[:, s, :, pl.ds(lat, 128)], keys.at[s, at, to, :, pl.ds(lat, 128)],
                    sems.at[k, s, 2 + i]))
        return out

    moving = [copies(s) for s in range(slots)]
    for group_of in moving:
        for c in group_of:
            c.start()
    for group_of in moving:
        for c in group_of:
            c.wait()
    zeros = count_zeros(slot_ref)
    factor = scale * math.log2(math.e)

    def put(o_ref, tile, slot, r):
        i = lax.broadcasted_iota(jnp.int32, (count, 1), 0)
        row = tile * TILE_ROWS + lax.rem(i, jnp.int32(TILE_ROWS))
        before = o_ref[tile].reshape(count, wide).astype(F32)
        o_ref[tile] = jnp.where((slot == 1) & (row < zeros), before, r).astype(BF).reshape(heads, per, wide)

    def chains(todo, slot, n, left):
        k = keys[slot, 0:n].reshape(n * block, wide)
        lane = lax.broadcasted_iota(jnp.int32, (count, block), 1)
        jobs = [(tile, q_ref, o_ref) for tile in todo for q_ref, o_ref in ((qa_ref, oa_ref), (qb_ref, ob_ref))]

        def scores_of(job):
            return lax.dot_general(
                job[1][job[0]].reshape(count, wide), k, (((1,), (1,)), ((), ())), preferred_element_type=F32)

        ahead = [scores_of(job) for job in jobs[:2]]
        for i, (tile, _, o_ref) in enumerate(jobs):
            if i + 2 < len(jobs):
                ahead.append(scores_of(jobs[i + 2]))
            s = ahead[i]
            last = jnp.where(lane < left, s[:, (n - 1) * block:], LOW)
            s = last if n == 1 else jnp.concatenate([s[:, :(n - 1) * block], last], axis=1)
            top = split2(jnp.max(s, axis=1, keepdims=True) * scale)
            p = jnp.exp2(s * factor - (top[0] + top[1]) * math.log2(math.e))
            total = jnp.sum(p, axis=1, keepdims=True)
            o = jnp.dot(p.astype(BF), k[:, :lat], preferred_element_type=F32)
            put(o_ref, tile, slot, partial_of(o, top, split2(total)))

    def one_slot(slot, carry):
        begin = jnp.where(slot == 0, 0, lax.div(zeros, jnp.int32(TILE_ROWS)))
        end = jnp.where(slot == 0, lax.div(zeros + (TILE_ROWS - 1), jnp.int32(TILE_ROWS)), tiles)
        length = len_ref[assign_ref[group * slots + slot]]
        prefix = lax.div(length - block * core + (2 * block - 1), jnp.int32(2 * block))
        blocks = sum(jnp.where(origin[k] < prefix, 1, 0) for k in shifts)
        final = functools.reduce(jnp.maximum, [jnp.where(origin[k] < prefix, origin[k], 0) for k in shifts])
        left = length - (2 * final + core) * block
        pairs = lax.div(end - begin, jnp.int32(2))

        @pl.when(blocks == 0)
        def _():
            nothing = partial_of(jnp.zeros((count, lat), F32), (jnp.full((count, 1), LOW, F32),), ())

            def fill(tile, c):
                put(oa_ref, tile, slot, nothing)
                put(ob_ref, tile, slot, nothing)
                return c

            lax.fori_loop(begin, end, fill, 0)

        for n in range(1, len(shifts) + 1):
            @pl.when(blocks == n)
            def _(n=n):
                def pair(i, c):
                    chains([begin + 2 * i, begin + 2 * i + 1], slot, n, left)
                    return c

                lax.fori_loop(0, pairs, pair, 0)

                @pl.when(begin + 2 * pairs < end)
                def _():
                    chains([end - 1], slot, n, left)
        return carry

    lax.fori_loop(0, slots, one_slot, 0)


def attend(layer, scale, shifts, row_slot, assign, prompt_len, qa, qb, pieces, ropes):
    tiles, heads, per, wide = qa.shape
    parts, slots, rows, _ = ropes[0].shape
    smem = pl.BlockSpec(memory_space=pltpu.SMEM)
    vmem = pl.BlockSpec(memory_space=pltpu.VMEM)
    held = list(pieces) + (list(ropes) if layer else [])
    shape = jax.ShapeDtypeStruct(qa.shape, BF)
    part = len(shifts)
    parts = parts if 2 not in shifts or part > 1 else 2 * parts
    return pl.pallas_call(
        functools.partial(attend_body, layer, scale, shifts),
        in_specs=[smem] * 3 + [vmem] * 2 + [pl.BlockSpec(memory_space=pl.ANY)] * len(held),
        out_specs=[vmem] * 2,
        out_shape=[shape, shape],
        scratch_shapes=[
            pltpu.VMEM((slots, part, parts, rows, wide), BF),
            pltpu.SemaphoreType.DMA((4, slots, 4)),
        ],
        compiler_params=params(32),
        cost_estimate=cost(2 * 2 * tiles * heads * per * part * parts * rows * 1152, 4 * qa.size * 2, 0),
        name="attend",
    )(row_slot, assign, prompt_len, qa, qb, *held)


def merge_body(layer, steps, count, slot_ref, w_ref, *refs):
    o_ref = refs[-1]
    partials = refs[:count]
    tiles, heads, per, wide = partials[0].shape
    lat = wide - 128
    total = tiles * per
    rows = o_ref.shape[2]
    value = w_ref.shape[3]

    places = row_places(slot_ref)
    sub = lax.broadcasted_iota(jnp.int32, (steps * rows, total), 0)
    step_of = sub // rows
    row_of = sub - step_of * rows
    where_to = jnp.full((steps * rows, total), -1, jnp.int32)
    for r in range(rows):
        where_to = jnp.where(row_of == r, places[r], where_to)
    place, step = order_index(1, (steps * rows, total), steps)
    back = jnp.where((place == where_to) & (step == step_of), 1.0, 0.0).astype(BF)

    lane = lax.broadcasted_iota(jnp.int32, (128, 128), 0)
    spread_top = jnp.where(lane < 2, 1.0, 0.0).astype(BF)
    spread_total = jnp.where((lane >= 2) & (lane < 4), 1.0, 0.0).astype(BF)
    every = tiles * heads * per
    tails = [r[:, :, :, lat:].reshape(every, 128) for r in partials]
    tops = [jnp.dot(v, spread_top, preferred_element_type=F32) for v in tails]
    totals = [jnp.dot(v, spread_total, preferred_element_type=F32) for v in tails]
    top = functools.reduce(jnp.maximum, tops)
    w = [jnp.exp(v - top) for v in tops]
    inv = 1.0 / sum(wi * v for wi, v in zip(w, totals))
    w = [wi * inv for wi in w]
    o = jnp.concatenate([
        sum(wi * r[:, :, :, c:c + 128].reshape(every, 128).astype(F32) for wi, r in zip(w, partials)).astype(BF)
        for c in range(0, lat, 128)
    ], axis=1).reshape(tiles, heads, per, lat)
    res = [
        jnp.dot(o[:, h].reshape(total, lat), w_ref[layer, h], preferred_element_type=F32).astype(BF)
        for h in range(heads)
    ]
    res = jnp.dot(back, jnp.concatenate(res, axis=1), preferred_element_type=F32).astype(BF)
    o_ref[:, 0] = res.reshape(steps, rows, heads * value)


def merge(layer, layers, steps, rows, row_slot, partials, w_uv, before):
    tiles, heads, per, wide = partials[0].shape
    lat, value = w_uv.shape[2:]
    vmem = pl.BlockSpec(memory_space=pltpu.VMEM)
    held = [] if before is None else [before]
    return pl.pallas_call(
        functools.partial(merge_body, layer, steps, len(partials)),
        grid=(1,),
        in_specs=[pl.BlockSpec(memory_space=pltpu.SMEM)] + [vmem] * (1 + len(partials))
        + [pl.BlockSpec(memory_space=pl.ANY)] * len(held),
        out_specs=pl.BlockSpec((steps, 1, rows, heads * value), lambda i: (0, layer, 0, 0)),
        out_shape=jax.ShapeDtypeStruct((steps, layers, rows, heads * value), BF),
        input_output_aliases={2 + len(partials): 0} if held else {},
        compiler_params=params(24),
        cost_estimate=cost(2 * tiles * per * heads * lat * value, len(partials) * partials[0].size * 2),
        name="merge",
    )(row_slot, w_uv, *partials, *held)


def local(n_section, n_head, kv_cache, prompt_len, assign, row_slot, q_nope, q_rope, new_kv, w_uk, w_uv):
    layers = kv_cache.shape[0]
    steps, _, rows, _ = q_nope.shape
    _, heads, nope, lat = w_uk.shape
    width = kv_cache.shape[3]
    rope = width - lat
    scale = (nope + rope) ** (-0.5)
    tiles = rows // TILE_ROWS
    chips = n_head // 2

    def spread(x):
        return lax.all_to_all(x, "section", 0, 0, tiled=True)

    def step_y(x, k):
        return lax.ppermute(x, "head", [(h, ((h // 2 + k) % chips) * 2 + h % 2) for h in range(n_head)])

    def onward(up, down):
        half = up.shape[0] // 2
        return [step_y(up[:half], 1), step_y(down[half:], -1)]

    def swap(x):
        return lax.ppermute(x, "head", [(h, h ^ 1) for h in range(n_head)])

    zero = jnp.zeros((steps, rows, rope), BF)
    nk = jnp.stack([
        jnp.concatenate([new_kv[:, 0], zero], axis=2),
        jnp.concatenate([new_kv[:, 1, :, :lat], zero, new_kv[:, 1, :, lat:]], axis=2),
    ], axis=1)
    qn = [queries(layer, tiles, scale, row_slot, q_nope, q_rope, w_uk, nk) for layer in range(layers)]
    sib = [swap(q) for q, _ in qn]

    x = spread(pack(kv_cache, n_section, lat))
    x, qn = lax.optimization_barrier((x, qn))
    k0, k1 = [spread(pick(layer, lat, assign, x)) for layer in range(layers)]
    k0, sib = lax.optimization_barrier((k0, sib))
    up, down = step_y(k0, 1), step_y(k0, -1)
    up, down, k1 = lax.optimization_barrier((up, down, k1))
    near0, far0 = [k0, up, down], onward(up, down)
    up, down = step_y(k1, 1), step_y(k1, -1)
    order = (0, 1, 3, 2)

    def attended(layer, shifts, pieces, ropes):
        return attend(layer, scale, shifts, row_slot, assign, prompt_len, qn[layer][0], sib[layer], pieces, ropes)

    first = attended(0, order[:3], near0, near0)
    first, up, down = lax.optimization_barrier((first, up, down))
    p1 = [k1, up, down] + onward(up, down)
    calls = [[first, attended(0, order[3:], far0, far0)], [attended(1, order, p1, near0 + far0)]]
    out = None
    for layer in range(layers):
        partials = [x for mine, theirs in calls[layer] for x in (mine, swap(theirs))]
        out = merge(layer, layers, steps, rows, row_slot, partials + [qn[layer][1]], w_uv, out)
    return out


def solution(mesh):
    in_specs = (
        P(None, "section", "head", None),
        P(),
        P(),
        P("section"),
        P(None, None, "section", "head"),
        P(None, None, "section", "head"),
        P(None, None, "section", None),
        P(None, "head", None, None),
        P(None, "head", None, None),
    )
    out_specs = P(None, None, "section", "head")
    step = functools.partial(local, mesh.shape["section"], mesh.shape["head"])
    return jax.shard_map(step, mesh=mesh, in_specs=in_specs, out_specs=out_specs, check_vma=False)
```

```python
import functools
import math

import jax
import jax.numpy as jnp
from jax import lax
from jax.experimental import pallas as pl
from jax.experimental.pallas import tpu as pltpu
from jax.sharding import PartitionSpec as P

BF = jnp.bfloat16
F32 = jnp.float32
TILE_ROWS = 8
LOW = -1e30
MIB = 1 << 20


def params(limit, **extra):
    return pltpu.CompilerParams(vmem_limit_bytes=limit * MIB, **extra)


def cost(flops, nbytes, trans=0):
    return pl.CostEstimate(flops=int(flops), bytes_accessed=int(nbytes), transcendentals=int(trans))


def pack_body(lat, kv_ref, x_ref):
    parts, _, rows, wide = x_ref.shape
    a = kv_ref[0, 0].T
    b = kv_ref[1, 0].T
    x = jnp.concatenate([a[:, :lat], b[:, :lat], a[:, lat:], b[:, lat:]], axis=1)
    x_ref[:, 0] = x.reshape(parts, rows, wide)


def pack(kv, parts, lat):
    layers, prompts, tok, width = kv.shape
    rows = tok // parts
    return pl.pallas_call(
        functools.partial(pack_body, lat),
        grid=(prompts,),
        in_specs=[pl.BlockSpec((layers, 1, width, tok), lambda p: (0, p, 0, 0))],
        out_specs=pl.BlockSpec((parts, 1, rows, layers * width), lambda p: (0, p, 0, 0)),
        out_shape=jax.ShapeDtypeStruct((parts, prompts, rows, layers * width), BF),
        compiler_params=params(16),
        cost_estimate=cost(0, 2 * kv.size * 2),
        name="pack",
    )(kv.transpose(0, 1, 3, 2))


def pick_body(layer, lat, assign_ref, x_ref, o_ref):
    for i in range(o_ref.shape[0]):
        p = assign_ref[i]
        o_ref[i, :, :lat] = x_ref[p, :, layer * lat:(layer + 1) * lat]
        if layer == 0:
            o_ref[i, :, lat:] = x_ref[p, :, 2 * lat:]


def pick(layer, lat, assign, x):
    groups, slots, rows, wide = x.shape
    out = lat if layer else wide - lat
    res = pl.pallas_call(
        functools.partial(pick_body, layer, lat),
        in_specs=[
            pl.BlockSpec(memory_space=pltpu.SMEM),
            pl.BlockSpec(memory_space=pltpu.VMEM),
        ],
        out_specs=pl.BlockSpec(memory_space=pltpu.VMEM),
        out_shape=jax.ShapeDtypeStruct((groups * slots, rows, out), BF),
        compiler_params=params(16),
        cost_estimate=cost(0, 2 * x.size * 2),
        name="pick",
    )(assign, x.reshape(groups * slots, rows, wide))
    return res.reshape(groups, slots, rows, out)


def count_zeros(slot_ref):
    zeros = jnp.int32(slot_ref.shape[0])
    for r in range(slot_ref.shape[0]):
        zeros = zeros - slot_ref[r]
    return zeros


def row_places(slot_ref):
    places = []
    c0, c1 = jnp.int32(0), count_zeros(slot_ref)
    for r in range(slot_ref.shape[0]):
        s = slot_ref[r]
        places.append(jnp.where(s == 0, c0, c1))
        c0 = c0 + (1 - s)
        c1 = c1 + s
    return places


def order_index(axis, shape, steps):
    i = lax.broadcasted_iota(jnp.int32, shape, axis)
    per = TILE_ROWS * steps
    tile = i // per
    rest = i - tile * per
    step = rest // TILE_ROWS
    return tile * TILE_ROWS + (rest - step * TILE_ROWS), step


def split2(x):
    hi = x.astype(BF).astype(F32)
    return hi, (x - hi).astype(BF).astype(F32)


def partial_of(o, top, total):
    lane = lax.broadcasted_iota(jnp.int32, (o.shape[0], 128), 1)
    tail = jnp.zeros((o.shape[0], 128), F32)
    for i, v in enumerate(top + total):
        tail = jnp.where(lane == i, v, tail)
    return jnp.concatenate([o, tail], axis=1)


def query_body(layer, steps, scale, slot_ref, nope_ref, rope_ref, w_ref, nk_ref, q_ref, n_ref, perm_ref, own_ref):
    tiles, heads, per, wide = q_ref.shape
    rows = nope_ref.shape[2]
    nope = w_ref.shape[2]
    lat = w_ref.shape[3]
    total = tiles * per

    @pl.when(pl.program_id(0) == 0)
    def _():
        places = row_places(slot_ref)
        lane = lax.broadcasted_iota(jnp.int32, (1, steps * rows), 1)
        step_of = lane // rows
        row_of = lane - step_of * rows
        where_to = jnp.full((1, steps * rows), -1, jnp.int32)
        for r in range(rows):
            where_to = jnp.where(row_of == r, places[r], where_to)
        place, step = order_index(0, (total, steps * rows), steps)
        perm_ref[...] = jnp.where((place == where_to) & (step == step_of), 1.0, 0.0).astype(BF)
        lane1 = lax.broadcasted_iota(jnp.int32, (total, rows), 1)
        place1, _ = order_index(0, (total, rows), steps)
        where1 = jnp.full((1, rows), -1, jnp.int32)
        lane_r = lax.broadcasted_iota(jnp.int32, (1, rows), 1)
        for r in range(rows):
            where1 = jnp.where(lane_r == r, places[r], where1)
        by_row = jnp.where(place1 == where1, 1.0, 0.0).astype(BF)
        for s in range(steps):
            own_ref[s] = jnp.dot(by_row, nk_ref[s, 0], preferred_element_type=F32)

    perm = perm_ref[...]
    x = nope_ref[:, 0].reshape(steps * rows, heads * nope)
    x = jnp.dot(perm, x, preferred_element_type=F32).astype(BF)
    r = rope_ref[:, 0].reshape(steps * rows, 128)
    r = jnp.dot(perm, r, preferred_element_type=F32)
    rolled = pltpu.roll(r, 64, 1)
    lane = lax.broadcasted_iota(jnp.int32, (total, 128), 1)
    mine = (lane // 64) == layer
    _, step = order_index(0, (total, 1), steps)
    for h in range(heads):
        ql = jnp.dot(x[:, h * nope:(h + 1) * nope], w_ref[0, h], preferred_element_type=F32).astype(BF)
        qr = jnp.where(mine, r if h == layer else rolled, 0.0).astype(BF)
        q = jnp.concatenate([ql, qr], axis=1)
        q_ref[:, h] = q.reshape(tiles, per, wide)
        qf = q.astype(F32)
        scores = []
        for s in range(steps):
            v = jnp.sum(qf * own_ref[s], axis=1, keepdims=True) * scale
            scores.append(jnp.where(step >= s, v, LOW))
        top = split2(functools.reduce(jnp.maximum, scores))
        weights = [jnp.exp(v - (top[0] + top[1])) for v in scores]
        o = weights[0] * own_ref[0, :, :lat]
        for s in range(1, steps):
            o = o + weights[s] * own_ref[s, :, :lat]
        part = partial_of(o, top, split2(sum(weights)))
        n_ref[:, h] = part.astype(BF).reshape(tiles, per, wide)


def queries(layer, tiles, scale, row_slot, q_nope, q_rope, w_uk, nk):
    steps, _, rows, _ = q_nope.shape
    _, heads, nope, lat = w_uk.shape
    wide = nk.shape[3]
    per = TILE_ROWS * steps
    shape = jax.ShapeDtypeStruct((tiles, heads, per, wide), BF)
    return pl.pallas_call(
        functools.partial(query_body, layer, steps, scale),
        grid=(heads // 2,),
        in_specs=[
            pl.BlockSpec(memory_space=pltpu.SMEM),
            pl.BlockSpec((steps, 1, rows, 2 * nope), lambda h: (0, layer, 0, h)),
            pl.BlockSpec((steps, 1, rows, 128), lambda h: (0, layer, 0, h)),
            pl.BlockSpec((1, 2, nope, lat), lambda h: (layer, h, 0, 0)),
            pl.BlockSpec((steps, 1, rows, wide), lambda h: (0, layer, 0, 0)),
        ],
        out_specs=[pl.BlockSpec((tiles, 2, per, wide), lambda h: (0, h, 0, 0))] * 2,
        out_shape=[shape, shape],
        scratch_shapes=[
            pltpu.VMEM((tiles * per, steps * rows), BF),
            pltpu.VMEM((steps, tiles * per, wide), F32),
        ],
        compiler_params=params(16),
        cost_estimate=cost(2 * tiles * per * heads * nope * lat, w_uk.size + 4 * tiles * per * heads * wide),
        name="queries",
    )(row_slot, q_nope, q_rope, w_uk, nk)


def attend_body(layer, scale, shifts, slot_ref, assign_ref, len_ref, qa_hbm, qb_hbm, *refs):
    names = [(k, i) for k in shifts for i in range(2 if k == 2 else 1)]
    pieces = refs[:len(names)]
    ropes = refs[len(names):2 * len(names)] if layer else None
    oa_ref, ob_ref, keys, qa_ref, qb_ref, sems, q_sems = refs[-7:]
    slots = keys.shape[0]
    group = lax.axis_index("section")
    head = lax.axis_index("head")
    y = lax.div(head, jnp.int32(2))
    core = lax.rem(head, jnp.int32(2))
    wide = keys.shape[-1]
    lat = wide - 128
    block = keys.shape[2] * keys.shape[3]
    tiles, heads, per, _ = oa_ref.shape
    count = heads * per
    half = keys.shape[2] // 2
    own = lat if layer else wide
    origin = {k: lax.rem(y - k + 4, jnp.int32(4)) for k in shifts}

    def copies(s):
        out = []
        for j, (k, i) in enumerate(names):
            at = sum(jnp.where(origin[o] < origin[k], 1, 0) for o in shifts)
            to = pl.ds(i * half, half) if k == 2 else pl.ds(0, 2 * half)
            out.append(pltpu.make_async_copy(
                pieces[j].at[:, s], keys.at[s, at, to, :, pl.ds(0, own)], sems.at[k, s, i]))
            if layer:
                out.append(pltpu.make_async_copy(
                    ropes[j].at[:, s, :, pl.ds(lat, 128)], keys.at[s, at, to, :, pl.ds(lat, 128)],
                    sems.at[k, s, 2 + i]))
        return out

    def query_copies(tile):
        return [
            pltpu.make_async_copy(held.at[tile], here.at[tile], q_sems.at[tile, i])
            for i, (held, here) in enumerate(((qa_hbm, qa_ref), (qb_hbm, qb_ref)))
        ]

    moving = [copies(s) for s in range(slots)]
    for c in moving[0] + query_copies(0) + moving[1]:
        c.start()
    for tile in range(1, tiles):
        for c in query_copies(tile):
            c.start()
    for c in moving[0] + moving[1]:
        c.wait()
    zeros = count_zeros(slot_ref)
    factor = scale * math.log2(math.e)

    def arrive(tile, slot):
        @pl.when((slot == 0) | (tile * TILE_ROWS >= zeros))
        def _():
            for c in query_copies(tile):
                c.wait()

    def put(o_ref, tile, slot, r):
        i = lax.broadcasted_iota(jnp.int32, (count, 1), 0)
        row = tile * TILE_ROWS + lax.rem(i, jnp.int32(TILE_ROWS))
        before = o_ref[tile].reshape(count, wide).astype(F32)
        o_ref[tile] = jnp.where((slot == 1) & (row < zeros), before, r).astype(BF).reshape(heads, per, wide)

    def chains(todo, slot, n, left):
        k = keys[slot, 0:n].reshape(n * block, wide)
        lane = lax.broadcasted_iota(jnp.int32, (count, block), 1)
        jobs = [(tile, q_ref, o_ref) for tile in todo for q_ref, o_ref in ((qa_ref, oa_ref), (qb_ref, ob_ref))]

        def scores_of(job):
            return lax.dot_general(
                job[1][job[0]].reshape(count, wide), k, (((1,), (1,)), ((), ())), preferred_element_type=F32)

        lead = 4 if n <= 2 else 2
        ahead = [scores_of(job) for job in jobs[:lead]]
        for i, (tile, _, o_ref) in enumerate(jobs):
            if i + lead < len(jobs):
                ahead.append(scores_of(jobs[i + lead]))
            s = ahead[i]
            last = jnp.where(lane < left, s[:, (n - 1) * block:], LOW)
            s = last if n == 1 else jnp.concatenate([s[:, :(n - 1) * block], last], axis=1)
            top = split2(jnp.max(s, axis=1, keepdims=True) * scale)
            p = jnp.exp2(s * factor - (top[0] + top[1]) * math.log2(math.e))
            total = jnp.sum(p, axis=1, keepdims=True)
            o = jnp.dot(p.astype(BF), k[:, :lat], preferred_element_type=F32)
            put(o_ref, tile, slot, partial_of(o, top, split2(total)))

    def one_slot(slot, carry):
        begin = jnp.where(slot == 0, 0, lax.div(zeros, jnp.int32(TILE_ROWS)))
        end = jnp.where(slot == 0, lax.div(zeros + (TILE_ROWS - 1), jnp.int32(TILE_ROWS)), tiles)
        length = len_ref[assign_ref[group * slots + slot]]
        prefix = lax.div(length - block * core + (2 * block - 1), jnp.int32(2 * block))
        blocks = sum(jnp.where(origin[k] < prefix, 1, 0) for k in shifts)
        final = functools.reduce(jnp.maximum, [jnp.where(origin[k] < prefix, origin[k], 0) for k in shifts])
        left = length - (2 * final + core) * block
        pairs = lax.div(end - begin, jnp.int32(2))

        @pl.when(blocks == 0)
        def _():
            nothing = partial_of(jnp.zeros((count, lat), F32), (jnp.full((count, 1), LOW, F32),), ())

            def fill(tile, c):
                arrive(tile, slot)
                put(oa_ref, tile, slot, nothing)
                put(ob_ref, tile, slot, nothing)
                return c

            lax.fori_loop(begin, end, fill, 0)

        for n in range(1, len(shifts) + 1):
            @pl.when(blocks == n)
            def _(n=n):
                def pair(i, c):
                    arrive(begin + 2 * i, slot)
                    arrive(begin + 2 * i + 1, slot)
                    chains([begin + 2 * i, begin + 2 * i + 1], slot, n, left)
                    return c

                lax.fori_loop(0, pairs, pair, 0)

                @pl.when(begin + 2 * pairs < end)
                def _():
                    arrive(end - 1, slot)
                    chains([end - 1], slot, n, left)
        return carry

    lax.fori_loop(0, slots, one_slot, 0)


def attend(layer, scale, shifts, row_slot, assign, prompt_len, qa, qb, pieces, ropes):
    tiles, heads, per, wide = qa.shape
    parts, slots, rows, _ = ropes[0].shape
    smem = pl.BlockSpec(memory_space=pltpu.SMEM)
    vmem = pl.BlockSpec(memory_space=pltpu.VMEM)
    held = list(pieces) + (list(ropes) if layer else [])
    shape = jax.ShapeDtypeStruct(qa.shape, BF)
    part = len(shifts)
    parts = parts if 2 not in shifts or part > 1 else 2 * parts
    return pl.pallas_call(
        functools.partial(attend_body, layer, scale, shifts),
        in_specs=[smem] * 3 + [pl.BlockSpec(memory_space=pl.ANY)] * (2 + len(held)),
        out_specs=[vmem] * 2,
        out_shape=[shape, shape],
        scratch_shapes=[
            pltpu.VMEM((slots, part, parts, rows, wide), BF),
            pltpu.VMEM(qa.shape, BF),
            pltpu.VMEM(qa.shape, BF),
            pltpu.SemaphoreType.DMA((4, slots, 4)),
            pltpu.SemaphoreType.DMA((tiles, 2)),
        ],
        compiler_params=params(32),
        cost_estimate=cost(2 * 2 * tiles * heads * per * part * parts * rows * 1152, 4 * qa.size * 2, 0),
        name="attend",
    )(row_slot, assign, prompt_len, qa, qb, *held)


def merge_body(layer, steps, count, slot_ref, w_ref, *refs):
    o_ref = refs[-1]
    partials = refs[:count]
    tiles, heads, per, wide = partials[0].shape
    lat = wide - 128
    total = tiles * per
    rows = o_ref.shape[2]
    value = w_ref.shape[3]

    places = row_places(slot_ref)
    sub = lax.broadcasted_iota(jnp.int32, (steps * rows, total), 0)
    step_of = sub // rows
    row_of = sub - step_of * rows
    where_to = jnp.full((steps * rows, total), -1, jnp.int32)
    for r in range(rows):
        where_to = jnp.where(row_of == r, places[r], where_to)
    place, step = order_index(1, (steps * rows, total), steps)
    back = jnp.where((place == where_to) & (step == step_of), 1.0, 0.0).astype(BF)

    lane = lax.broadcasted_iota(jnp.int32, (128, 128), 0)
    spread_top = jnp.where(lane < 2, 1.0, 0.0).astype(BF)
    spread_total = jnp.where((lane >= 2) & (lane < 4), 1.0, 0.0).astype(BF)
    every = tiles * heads * per
    tails = [r[:, :, :, lat:].reshape(every, 128) for r in partials]
    tops = [jnp.dot(v, spread_top, preferred_element_type=F32) for v in tails]
    totals = [jnp.dot(v, spread_total, preferred_element_type=F32) for v in tails]
    top = functools.reduce(jnp.maximum, tops)
    w = [jnp.exp(v - top) for v in tops]
    inv = 1.0 / sum(wi * v for wi, v in zip(w, totals))
    w = [wi * inv for wi in w]
    o = jnp.concatenate([
        sum(wi * r[:, :, :, c:c + 128].reshape(every, 128).astype(F32) for wi, r in zip(w, partials)).astype(BF)
        for c in range(0, lat, 128)
    ], axis=1).reshape(tiles, heads, per, lat)
    res = [
        jnp.dot(o[:, h].reshape(total, lat), w_ref[layer, h], preferred_element_type=F32).astype(BF)
        for h in range(heads)
    ]
    res = jnp.dot(back, jnp.concatenate(res, axis=1), preferred_element_type=F32).astype(BF)
    o_ref[:, 0] = res.reshape(steps, rows, heads * value)


def merge(layer, layers, steps, rows, row_slot, partials, w_uv, before):
    tiles, heads, per, wide = partials[0].shape
    lat, value = w_uv.shape[2:]
    vmem = pl.BlockSpec(memory_space=pltpu.VMEM)
    held = [] if before is None else [before]
    return pl.pallas_call(
        functools.partial(merge_body, layer, steps, len(partials)),
        grid=(1,),
        in_specs=[pl.BlockSpec(memory_space=pltpu.SMEM)] + [vmem] * (1 + len(partials))
        + [pl.BlockSpec(memory_space=pl.ANY)] * len(held),
        out_specs=pl.BlockSpec((steps, 1, rows, heads * value), lambda i: (0, layer, 0, 0)),
        out_shape=jax.ShapeDtypeStruct((steps, layers, rows, heads * value), BF),
        input_output_aliases={2 + len(partials): 0} if held else {},
        compiler_params=params(24),
        cost_estimate=cost(2 * tiles * per * heads * lat * value, len(partials) * partials[0].size * 2),
        name="merge",
    )(row_slot, w_uv, *partials, *held)


def local(n_section, n_head, kv_cache, prompt_len, assign, row_slot, q_nope, q_rope, new_kv, w_uk, w_uv):
    layers = kv_cache.shape[0]
    steps, _, rows, _ = q_nope.shape
    _, heads, nope, lat = w_uk.shape
    width = kv_cache.shape[3]
    rope = width - lat
    scale = (nope + rope) ** (-0.5)
    tiles = rows // TILE_ROWS
    chips = n_head // 2

    def spread(x):
        return lax.all_to_all(x, "section", 0, 0, tiled=True)

    def step_y(x, k):
        return lax.ppermute(x, "head", [(h, ((h // 2 + k) % chips) * 2 + h % 2) for h in range(n_head)])

    def onward(up, down):
        half = up.shape[0] // 2
        return [step_y(up[:half], 1), step_y(down[half:], -1)]

    def swap(x):
        return lax.ppermute(x, "head", [(h, h ^ 1) for h in range(n_head)])

    zero = jnp.zeros((steps, rows, rope), BF)
    nk = jnp.stack([
        jnp.concatenate([new_kv[:, 0], zero], axis=2),
        jnp.concatenate([new_kv[:, 1, :, :lat], zero, new_kv[:, 1, :, lat:]], axis=2),
    ], axis=1)
    qn = [queries(layer, tiles, scale, row_slot, q_nope, q_rope, w_uk, nk) for layer in range(layers)]
    sib = [swap(q) for q, _ in qn]

    x = spread(pack(kv_cache, n_section, lat))
    x, qn = lax.optimization_barrier((x, qn))
    picked = [pick(layer, lat, assign, x) for layer in range(layers)]
    k0, sib, later = lax.optimization_barrier((spread(picked[0]), sib, picked[1]))
    k1 = spread(later)
    up, down = step_y(k0, 1), step_y(k0, -1)
    up, down, k1 = lax.optimization_barrier((up, down, k1))
    near0, far0 = [k0, up, down], onward(up, down)
    up, down = step_y(k1, 1), step_y(k1, -1)
    order = (0, 1, 3, 2)

    def attended(layer, shifts, pieces, ropes):
        return attend(layer, scale, shifts, row_slot, assign, prompt_len, qn[layer][0], sib[layer], pieces, ropes)

    first = attended(0, order[:3], near0, near0)
    first, up, down = lax.optimization_barrier((first, up, down))
    p1 = [k1, up, down] + onward(up, down)
    calls = [[first, attended(0, order[3:], far0, far0)], [attended(1, order, p1, near0 + far0)]]
    out = None
    for layer in range(layers):
        partials = [x for mine, theirs in calls[layer] for x in (mine, swap(theirs))]
        out = merge(layer, layers, steps, rows, row_slot, partials + [qn[layer][1]], w_uv, out)
    return out


def solution(mesh):
    in_specs = (
        P(None, "section", "head", None),
        P(),
        P(),
        P("section"),
        P(None, None, "section", "head"),
        P(None, None, "section", "head"),
        P(None, None, "section", None),
        P(None, "head", None, None),
        P(None, "head", None, None),
    )
    out_specs = P(None, None, "section", "head")
    step = functools.partial(local, mesh.shape["section"], mesh.shape["head"])
    return jax.shard_map(step, mesh=mesh, in_specs=in_specs, out_specs=out_specs, check_vma=False)
```

```python
import functools
import math

import jax
import jax.numpy as jnp
from jax import lax
from jax.experimental import pallas as pl
from jax.experimental.pallas import tpu as pltpu
from jax.sharding import PartitionSpec as P

BF = jnp.bfloat16
F32 = jnp.float32
TILE_ROWS = 8
LOW = -1e30
MIB = 1 << 20


def params(limit, **extra):
    return pltpu.CompilerParams(vmem_limit_bytes=limit * MIB, **extra)


def cost(flops, nbytes, trans=0):
    return pl.CostEstimate(flops=int(flops), bytes_accessed=int(nbytes), transcendentals=int(trans))


def pack_body(lat, kv_ref, x_ref):
    parts, _, rows, wide = x_ref.shape
    a = kv_ref[0, 0].T
    b = kv_ref[1, 0].T
    x = jnp.concatenate([a[:, :lat], b[:, :lat], a[:, lat:], b[:, lat:]], axis=1)
    x_ref[:, 0] = x.reshape(parts, rows, wide)


def pack(kv, parts, lat):
    layers, prompts, tok, width = kv.shape
    rows = tok // parts
    return pl.pallas_call(
        functools.partial(pack_body, lat),
        grid=(prompts,),
        in_specs=[pl.BlockSpec((layers, 1, width, tok), lambda p: (0, p, 0, 0))],
        out_specs=pl.BlockSpec((parts, 1, rows, layers * width), lambda p: (0, p, 0, 0)),
        out_shape=jax.ShapeDtypeStruct((parts, prompts, rows, layers * width), BF),
        compiler_params=params(16),
        cost_estimate=cost(0, 2 * kv.size * 2),
        name="pack",
    )(kv.transpose(0, 1, 3, 2))


def pick_body(layer, lat, assign_ref, x_ref, o_ref):
    for i in range(o_ref.shape[0]):
        p = assign_ref[i]
        o_ref[i, :, :lat] = x_ref[p, :, layer * lat:(layer + 1) * lat]
        if layer == 0:
            o_ref[i, :, lat:] = x_ref[p, :, 2 * lat:]


def pick(layer, lat, assign, x):
    groups, slots, rows, wide = x.shape
    out = lat if layer else wide - lat
    res = pl.pallas_call(
        functools.partial(pick_body, layer, lat),
        in_specs=[
            pl.BlockSpec(memory_space=pltpu.SMEM),
            pl.BlockSpec(memory_space=pltpu.VMEM),
        ],
        out_specs=pl.BlockSpec(memory_space=pltpu.VMEM),
        out_shape=jax.ShapeDtypeStruct((groups * slots, rows, out), BF),
        compiler_params=params(16),
        cost_estimate=cost(0, 2 * x.size * 2),
        name="pick",
    )(assign, x.reshape(groups * slots, rows, wide))
    return res.reshape(groups, slots, rows, out)


def count_zeros(slot_ref):
    zeros = jnp.int32(slot_ref.shape[0])
    for r in range(slot_ref.shape[0]):
        zeros = zeros - slot_ref[r]
    return zeros


def row_places(slot_ref):
    places = []
    c0, c1 = jnp.int32(0), count_zeros(slot_ref)
    for r in range(slot_ref.shape[0]):
        s = slot_ref[r]
        places.append(jnp.where(s == 0, c0, c1))
        c0 = c0 + (1 - s)
        c1 = c1 + s
    return places


def order_index(axis, shape, steps):
    i = lax.broadcasted_iota(jnp.int32, shape, axis)
    per = TILE_ROWS * steps
    tile = i // per
    rest = i - tile * per
    step = rest // TILE_ROWS
    return tile * TILE_ROWS + (rest - step * TILE_ROWS), step


def split2(x):
    hi = x.astype(BF).astype(F32)
    return hi, (x - hi).astype(BF).astype(F32)


def partial_of(o, top, total):
    lane = lax.broadcasted_iota(jnp.int32, (o.shape[0], 128), 1)
    tail = jnp.zeros((o.shape[0], 128), F32)
    for i, v in enumerate(top + total):
        tail = jnp.where(lane == i, v, tail)
    return jnp.concatenate([o, tail], axis=1)


def query_body(layer, steps, scale, slot_ref, nope_ref, rope_ref, w_ref, nk_ref, q_ref, n_ref, perm_ref, own_ref):
    tiles, heads, per, wide = q_ref.shape
    rows = nope_ref.shape[2]
    nope = w_ref.shape[2]
    lat = w_ref.shape[3]
    total = tiles * per

    @pl.when(pl.program_id(0) == 0)
    def _():
        places = row_places(slot_ref)
        lane = lax.broadcasted_iota(jnp.int32, (1, steps * rows), 1)
        step_of = lane // rows
        row_of = lane - step_of * rows
        where_to = jnp.full((1, steps * rows), -1, jnp.int32)
        for r in range(rows):
            where_to = jnp.where(row_of == r, places[r], where_to)
        place, step = order_index(0, (total, steps * rows), steps)
        perm_ref[...] = jnp.where((place == where_to) & (step == step_of), 1.0, 0.0).astype(BF)
        lane1 = lax.broadcasted_iota(jnp.int32, (total, rows), 1)
        place1, _ = order_index(0, (total, rows), steps)
        where1 = jnp.full((1, rows), -1, jnp.int32)
        lane_r = lax.broadcasted_iota(jnp.int32, (1, rows), 1)
        for r in range(rows):
            where1 = jnp.where(lane_r == r, places[r], where1)
        by_row = jnp.where(place1 == where1, 1.0, 0.0).astype(BF)
        for s in range(steps):
            own_ref[s] = jnp.dot(by_row, nk_ref[s, 0], preferred_element_type=F32)

    perm = perm_ref[...]
    x = nope_ref[:, 0].reshape(steps * rows, heads * nope)
    x = jnp.dot(perm, x, preferred_element_type=F32).astype(BF)
    r = rope_ref[:, 0].reshape(steps * rows, 128)
    r = jnp.dot(perm, r, preferred_element_type=F32)
    rolled = pltpu.roll(r, 64, 1)
    lane = lax.broadcasted_iota(jnp.int32, (total, 128), 1)
    mine = (lane // 64) == layer
    _, step = order_index(0, (total, 1), steps)
    for h in range(heads):
        ql = jnp.dot(x[:, h * nope:(h + 1) * nope], w_ref[0, h], preferred_element_type=F32).astype(BF)
        qr = jnp.where(mine, r if h == layer else rolled, 0.0).astype(BF)
        q = jnp.concatenate([ql, qr], axis=1)
        q_ref[:, h] = q.reshape(tiles, per, wide)
        qf = q.astype(F32)
        scores = []
        for s in range(steps):
            v = jnp.sum(qf * own_ref[s], axis=1, keepdims=True) * scale
            scores.append(jnp.where(step >= s, v, LOW))
        top = split2(functools.reduce(jnp.maximum, scores))
        weights = [jnp.exp(v - (top[0] + top[1])) for v in scores]
        o = weights[0] * own_ref[0, :, :lat]
        for s in range(1, steps):
            o = o + weights[s] * own_ref[s, :, :lat]
        part = partial_of(o, top, split2(sum(weights)))
        n_ref[:, h] = part.astype(BF).reshape(tiles, per, wide)


def queries(layer, tiles, scale, row_slot, q_nope, q_rope, w_uk, nk):
    steps, _, rows, _ = q_nope.shape
    _, heads, nope, lat = w_uk.shape
    wide = nk.shape[3]
    per = TILE_ROWS * steps
    shape = jax.ShapeDtypeStruct((tiles, heads, per, wide), BF)
    return pl.pallas_call(
        functools.partial(query_body, layer, steps, scale),
        grid=(heads // 2,),
        in_specs=[
            pl.BlockSpec(memory_space=pltpu.SMEM),
            pl.BlockSpec((steps, 1, rows, 2 * nope), lambda h: (0, layer, 0, h)),
            pl.BlockSpec((steps, 1, rows, 128), lambda h: (0, layer, 0, h)),
            pl.BlockSpec((1, 2, nope, lat), lambda h: (layer, h, 0, 0)),
            pl.BlockSpec((steps, 1, rows, wide), lambda h: (0, layer, 0, 0)),
        ],
        out_specs=[pl.BlockSpec((tiles, 2, per, wide), lambda h: (0, h, 0, 0))] * 2,
        out_shape=[shape, shape],
        scratch_shapes=[
            pltpu.VMEM((tiles * per, steps * rows), BF),
            pltpu.VMEM((steps, tiles * per, wide), F32),
        ],
        compiler_params=params(16),
        cost_estimate=cost(2 * tiles * per * heads * nope * lat, w_uk.size + 4 * tiles * per * heads * wide),
        name="queries",
    )(row_slot, q_nope, q_rope, w_uk, nk)


def attend_body(layer, scale, shifts, slot_ref, assign_ref, len_ref, qa_hbm, qb_hbm, *refs):
    names = [(k, i) for k in shifts for i in range(2 if k == 2 else 1)]
    pieces = refs[:len(names)]
    ropes = refs[len(names):2 * len(names)] if layer else None
    oa_ref, ob_ref, keys, qa_ref, qb_ref, kept, sems, q_sems = refs[-8:]
    slots = keys.shape[0]
    group = lax.axis_index("section")
    head = lax.axis_index("head")
    y = lax.div(head, jnp.int32(2))
    core = lax.rem(head, jnp.int32(2))
    wide = keys.shape[-1]
    lat = wide - 128
    block = keys.shape[2] * keys.shape[3]
    tiles, heads, per, _ = oa_ref.shape
    count = heads * per
    half = keys.shape[2] // 2
    own = lat if layer else wide
    origin = {k: lax.rem(y - k + 4, jnp.int32(4)) for k in shifts}

    def copies(s):
        out = []
        for j, (k, i) in enumerate(names):
            at = sum(jnp.where(origin[o] < origin[k], 1, 0) for o in shifts)
            to = pl.ds(i * half, half) if k == 2 else pl.ds(0, 2 * half)
            out.append(pltpu.make_async_copy(
                pieces[j].at[:, s], keys.at[s, at, to, :, pl.ds(0, own)], sems.at[k, s, i]))
            if layer:
                out.append(pltpu.make_async_copy(
                    ropes[j].at[:, s, :, pl.ds(lat, 128)], keys.at[s, at, to, :, pl.ds(lat, 128)],
                    sems.at[k, s, 2 + i]))
        return out

    def query_copies(tile):
        return [
            pltpu.make_async_copy(held.at[tile], here.at[tile], q_sems.at[tile, i])
            for i, (held, here) in enumerate(((qa_hbm, qa_ref), (qb_hbm, qb_ref)))
        ]

    moving = [copies(s) for s in range(slots)]
    for c in moving[0] + query_copies(0) + moving[1]:
        c.start()
    for tile in range(1, tiles):
        for c in query_copies(tile):
            c.start()
    for c in moving[0] + moving[1]:
        c.wait()
    zeros = count_zeros(slot_ref)
    factor = scale * math.log2(math.e)

    def arrive(tile, slot):
        @pl.when((slot == 0) | (tile * TILE_ROWS >= zeros))
        def _():
            for c in query_copies(tile):
                c.wait()

    def put(o_ref, tile, r):
        o_ref[tile] = r.astype(BF).reshape(heads, per, wide)

    def chains(todo, slot, n, left):
        k = keys[slot, 0:n].reshape(n * block, wide)
        lane = lax.broadcasted_iota(jnp.int32, (count, block), 1)
        jobs = [(tile, q_ref, o_ref) for tile in todo for q_ref, o_ref in ((qa_ref, oa_ref), (qb_ref, ob_ref))]

        def scores_of(job):
            return lax.dot_general(
                job[1][job[0]].reshape(count, wide), k, (((1,), (1,)), ((), ())), preferred_element_type=F32)

        lead = 4 if n <= 2 else 2
        ahead = [scores_of(job) for job in jobs[:lead]]
        for i, (tile, _, o_ref) in enumerate(jobs):
            if i + lead < len(jobs):
                ahead.append(scores_of(jobs[i + lead]))
            s = ahead[i]
            last = jnp.where(lane < left, s[:, (n - 1) * block:], LOW)
            s = last if n == 1 else jnp.concatenate([s[:, :(n - 1) * block], last], axis=1)
            top = split2(jnp.max(s, axis=1, keepdims=True) * scale)
            p = jnp.exp2(s * factor - (top[0] + top[1]) * math.log2(math.e))
            total = jnp.sum(p, axis=1, keepdims=True)
            o = jnp.dot(p.astype(BF), k[:, :lat], preferred_element_type=F32)
            put(o_ref, tile, partial_of(o, top, split2(total)))

    def one_slot(slot, carry):
        begin = jnp.where(slot == 0, 0, lax.div(zeros, jnp.int32(TILE_ROWS)))
        end = jnp.where(slot == 0, lax.div(zeros + (TILE_ROWS - 1), jnp.int32(TILE_ROWS)), tiles)
        length = len_ref[assign_ref[group * slots + slot]]
        prefix = lax.div(length - block * core + (2 * block - 1), jnp.int32(2 * block))
        blocks = sum(jnp.where(origin[k] < prefix, 1, 0) for k in shifts)
        final = functools.reduce(jnp.maximum, [jnp.where(origin[k] < prefix, origin[k], 0) for k in shifts])
        left = length - (2 * final + core) * block
        pairs = lax.div(end - begin, jnp.int32(2))
        shared = (slot == 1) & (begin * TILE_ROWS < zeros)

        @pl.when(shared)
        def _():
            kept[0] = oa_ref[begin]
            kept[1] = ob_ref[begin]

        @pl.when(blocks == 0)
        def _():
            nothing = partial_of(jnp.zeros((count, lat), F32), (jnp.full((count, 1), LOW, F32),), ())

            def fill(tile, c):
                arrive(tile, slot)
                put(oa_ref, tile, nothing)
                put(ob_ref, tile, nothing)
                return c

            lax.fori_loop(begin, end, fill, 0)

        for n in range(1, len(shifts) + 1):
            @pl.when(blocks == n)
            def _(n=n):
                def pair(i, c):
                    arrive(begin + 2 * i, slot)
                    arrive(begin + 2 * i + 1, slot)
                    chains([begin + 2 * i, begin + 2 * i + 1], slot, n, left)
                    return c

                lax.fori_loop(0, pairs, pair, 0)

                @pl.when(begin + 2 * pairs < end)
                def _():
                    arrive(end - 1, slot)
                    chains([end - 1], slot, n, left)

        @pl.when(shared)
        def _():
            i = lax.broadcasted_iota(jnp.int32, (count, 1), 0)
            before = begin * TILE_ROWS + lax.rem(i, jnp.int32(TILE_ROWS)) < zeros
            for old, o_ref in enumerate((oa_ref, ob_ref)):
                a = kept[old].reshape(count, wide).astype(F32)
                b = o_ref[begin].reshape(count, wide).astype(F32)
                put(o_ref, begin, jnp.where(before, a, b))
        return carry

    lax.fori_loop(0, slots, one_slot, 0)


def attend(layer, scale, shifts, row_slot, assign, prompt_len, qa, qb, pieces, ropes):
    tiles, heads, per, wide = qa.shape
    parts, slots, rows, _ = ropes[0].shape
    smem = pl.BlockSpec(memory_space=pltpu.SMEM)
    vmem = pl.BlockSpec(memory_space=pltpu.VMEM)
    held = list(pieces) + (list(ropes) if layer else [])
    shape = jax.ShapeDtypeStruct(qa.shape, BF)
    part = len(shifts)
    parts = parts if 2 not in shifts or part > 1 else 2 * parts
    return pl.pallas_call(
        functools.partial(attend_body, layer, scale, shifts),
        in_specs=[smem] * 3 + [pl.BlockSpec(memory_space=pl.ANY)] * (2 + len(held)),
        out_specs=[vmem] * 2,
        out_shape=[shape, shape],
        scratch_shapes=[
            pltpu.VMEM((slots, part, parts, rows, wide), BF),
            pltpu.VMEM(qa.shape, BF),
            pltpu.VMEM(qa.shape, BF),
            pltpu.VMEM((2, heads, per, wide), BF),
            pltpu.SemaphoreType.DMA((4, slots, 4)),
            pltpu.SemaphoreType.DMA((tiles, 2)),
        ],
        compiler_params=params(32),
        cost_estimate=cost(2 * 2 * tiles * heads * per * part * parts * rows * 1152, 4 * qa.size * 2, 0),
        name="attend",
    )(row_slot, assign, prompt_len, qa, qb, *held)


def merge_body(layer, steps, count, slot_ref, w_ref, *refs):
    o_ref = refs[-1]
    partials = refs[:count]
    tiles, heads, per, wide = partials[0].shape
    lat = wide - 128
    total = tiles * per
    rows = o_ref.shape[2]
    value = w_ref.shape[3]

    places = row_places(slot_ref)
    sub = lax.broadcasted_iota(jnp.int32, (steps * rows, total), 0)
    step_of = sub // rows
    row_of = sub - step_of * rows
    where_to = jnp.full((steps * rows, total), -1, jnp.int32)
    for r in range(rows):
        where_to = jnp.where(row_of == r, places[r], where_to)
    place, step = order_index(1, (steps * rows, total), steps)
    back = jnp.where((place == where_to) & (step == step_of), 1.0, 0.0).astype(BF)

    lane = lax.broadcasted_iota(jnp.int32, (128, 128), 0)
    spread_top = jnp.where(lane < 2, 1.0, 0.0).astype(BF)
    spread_total = jnp.where((lane >= 2) & (lane < 4), 1.0, 0.0).astype(BF)
    every = tiles * heads * per
    tails = [r[:, :, :, lat:].reshape(every, 128) for r in partials]
    tops = [jnp.dot(v, spread_top, preferred_element_type=F32) for v in tails]
    totals = [jnp.dot(v, spread_total, preferred_element_type=F32) for v in tails]
    top = functools.reduce(jnp.maximum, tops)
    w = [jnp.exp(v - top) for v in tops]
    inv = 1.0 / sum(wi * v for wi, v in zip(w, totals))
    w = [wi * inv for wi in w]
    o = jnp.concatenate([
        sum(wi * r[:, :, :, c:c + 128].reshape(every, 128).astype(F32) for wi, r in zip(w, partials)).astype(BF)
        for c in range(0, lat, 128)
    ], axis=1).reshape(tiles, heads, per, lat)
    res = [
        jnp.dot(o[:, h].reshape(total, lat), w_ref[layer, h], preferred_element_type=F32).astype(BF)
        for h in range(heads)
    ]
    res = jnp.dot(back, jnp.concatenate(res, axis=1), preferred_element_type=F32).astype(BF)
    o_ref[:, 0] = res.reshape(steps, rows, heads * value)


def merge(layer, layers, steps, rows, row_slot, partials, w_uv, before):
    tiles, heads, per, wide = partials[0].shape
    lat, value = w_uv.shape[2:]
    vmem = pl.BlockSpec(memory_space=pltpu.VMEM)
    held = [] if before is None else [before]
    return pl.pallas_call(
        functools.partial(merge_body, layer, steps, len(partials)),
        grid=(1,),
        in_specs=[pl.BlockSpec(memory_space=pltpu.SMEM)] + [vmem] * (1 + len(partials))
        + [pl.BlockSpec(memory_space=pl.ANY)] * len(held),
        out_specs=pl.BlockSpec((steps, 1, rows, heads * value), lambda i: (0, layer, 0, 0)),
        out_shape=jax.ShapeDtypeStruct((steps, layers, rows, heads * value), BF),
        input_output_aliases={2 + len(partials): 0} if held else {},
        compiler_params=params(24),
        cost_estimate=cost(2 * tiles * per * heads * lat * value, len(partials) * partials[0].size * 2),
        name="merge",
    )(row_slot, w_uv, *partials, *held)


def local(n_section, n_head, kv_cache, prompt_len, assign, row_slot, q_nope, q_rope, new_kv, w_uk, w_uv):
    layers = kv_cache.shape[0]
    steps, _, rows, _ = q_nope.shape
    _, heads, nope, lat = w_uk.shape
    width = kv_cache.shape[3]
    rope = width - lat
    scale = (nope + rope) ** (-0.5)
    tiles = rows // TILE_ROWS
    chips = n_head // 2

    def spread(x):
        return lax.all_to_all(x, "section", 0, 0, tiled=True)

    def step_y(x, k):
        return lax.ppermute(x, "head", [(h, ((h // 2 + k) % chips) * 2 + h % 2) for h in range(n_head)])

    def onward(up, down):
        half = up.shape[0] // 2
        return [step_y(up[:half], 1), step_y(down[half:], -1)]

    def swap(x):
        return lax.ppermute(x, "head", [(h, h ^ 1) for h in range(n_head)])

    zero = jnp.zeros((steps, rows, rope), BF)
    nk = jnp.stack([
        jnp.concatenate([new_kv[:, 0], zero], axis=2),
        jnp.concatenate([new_kv[:, 1, :, :lat], zero, new_kv[:, 1, :, lat:]], axis=2),
    ], axis=1)
    qn = [queries(layer, tiles, scale, row_slot, q_nope, q_rope, w_uk, nk) for layer in range(layers)]
    sib = [swap(q) for q, _ in qn]

    x = spread(pack(kv_cache, n_section, lat))
    x, qn = lax.optimization_barrier((x, qn))
    picked = [pick(layer, lat, assign, x) for layer in range(layers)]
    k0, sib, later = lax.optimization_barrier((spread(picked[0]), sib, picked[1]))
    k1 = spread(later)
    up, down = step_y(k0, 1), step_y(k0, -1)
    up, down, k1 = lax.optimization_barrier((up, down, k1))
    near0, far0 = [k0, up, down], onward(up, down)
    up, down = step_y(k1, 1), step_y(k1, -1)
    order = (0, 1, 3, 2)

    def attended(layer, shifts, pieces, ropes):
        return attend(layer, scale, shifts, row_slot, assign, prompt_len, qn[layer][0], sib[layer], pieces, ropes)

    first = attended(0, order[:3], near0, near0)
    first, up, down = lax.optimization_barrier((first, up, down))
    p1 = [k1, up, down] + onward(up, down)
    calls = [[first, attended(0, order[3:], far0, far0)], [attended(1, order, p1, near0 + far0)]]
    out = None
    for layer in range(layers):
        partials = [x for mine, theirs in calls[layer] for x in (mine, swap(theirs))]
        out = merge(layer, layers, steps, rows, row_slot, partials + [qn[layer][1]], w_uv, out)
    return out


def solution(mesh):
    in_specs = (
        P(None, "section", "head", None),
        P(),
        P(),
        P("section"),
        P(None, None, "section", "head"),
        P(None, None, "section", "head"),
        P(None, None, "section", None),
        P(None, "head", None, None),
        P(None, "head", None, None),
    )
    out_specs = P(None, None, "section", "head")
    step = functools.partial(local, mesh.shape["section"], mesh.shape["head"])
    return jax.shard_map(step, mesh=mesh, in_specs=in_specs, out_specs=out_specs, check_vma=False)
```

```python
import functools
import math

import jax
import jax.numpy as jnp
from jax import lax
from jax.experimental import pallas as pl
from jax.experimental.pallas import tpu as pltpu
from jax.sharding import PartitionSpec as P

BF = jnp.bfloat16
F32 = jnp.float32
TILE_ROWS = 8
LOW = -1e30
MIB = 1 << 20


def params(limit, **extra):
    return pltpu.CompilerParams(vmem_limit_bytes=limit * MIB, **extra)


def cost(flops, nbytes, trans=0):
    return pl.CostEstimate(flops=int(flops), bytes_accessed=int(nbytes), transcendentals=int(trans))


def pack_body(lat, kv_ref, x_ref):
    parts, _, rows, wide = x_ref.shape
    a = kv_ref[0, 0].T
    b = kv_ref[1, 0].T
    x = jnp.concatenate([a[:, :lat], b[:, :lat], a[:, lat:], b[:, lat:]], axis=1)
    x_ref[:, 0] = x.reshape(parts, rows, wide)


def pack(kv, parts, lat):
    layers, prompts, tok, width = kv.shape
    rows = tok // parts
    return pl.pallas_call(
        functools.partial(pack_body, lat),
        grid=(prompts,),
        in_specs=[pl.BlockSpec((layers, 1, width, tok), lambda p: (0, p, 0, 0))],
        out_specs=pl.BlockSpec((parts, 1, rows, layers * width), lambda p: (0, p, 0, 0)),
        out_shape=jax.ShapeDtypeStruct((parts, prompts, rows, layers * width), BF),
        compiler_params=params(60),
        cost_estimate=cost(0, 2 * kv.size * 2),
        name="pack",
    )(kv.transpose(0, 1, 3, 2))


def pick_body(layer, lat, assign_ref, x_ref, o_ref):
    for i in range(o_ref.shape[0]):
        p = assign_ref[i]
        o_ref[i, :, :lat] = x_ref[p, :, layer * lat:(layer + 1) * lat]
        if layer == 0:
            o_ref[i, :, lat:] = x_ref[p, :, 2 * lat:]


def pick(layer, lat, assign, x):
    groups, slots, rows, wide = x.shape
    out = lat if layer else wide - lat
    res = pl.pallas_call(
        functools.partial(pick_body, layer, lat),
        in_specs=[
            pl.BlockSpec(memory_space=pltpu.SMEM),
            pl.BlockSpec(memory_space=pltpu.VMEM),
        ],
        out_specs=pl.BlockSpec(memory_space=pltpu.VMEM),
        out_shape=jax.ShapeDtypeStruct((groups * slots, rows, out), BF),
        compiler_params=params(16),
        cost_estimate=cost(0, 2 * x.size * 2),
        name="pick",
    )(assign, x.reshape(groups * slots, rows, wide))
    return res.reshape(groups, slots, rows, out)


def count_zeros(slot_ref):
    zeros = jnp.int32(slot_ref.shape[0])
    for r in range(slot_ref.shape[0]):
        zeros = zeros - slot_ref[r]
    return zeros


def row_places(slot_ref):
    places = []
    c0, c1 = jnp.int32(0), count_zeros(slot_ref)
    for r in range(slot_ref.shape[0]):
        s = slot_ref[r]
        places.append(jnp.where(s == 0, c0, c1))
        c0 = c0 + (1 - s)
        c1 = c1 + s
    return places


def order_index(axis, shape, steps):
    i = lax.broadcasted_iota(jnp.int32, shape, axis)
    per = TILE_ROWS * steps
    tile = i // per
    rest = i - tile * per
    step = rest // TILE_ROWS
    return tile * TILE_ROWS + (rest - step * TILE_ROWS), step


def split2(x):
    hi = x.astype(BF).astype(F32)
    return hi, (x - hi).astype(BF).astype(F32)


def partial_of(o, top, total):
    lane = lax.broadcasted_iota(jnp.int32, (o.shape[0], 128), 1)
    tail = jnp.zeros((o.shape[0], 128), F32)
    for i, v in enumerate(top + total):
        tail = jnp.where(lane == i, v, tail)
    return jnp.concatenate([o, tail], axis=1)


def query_body(layer, steps, scale, slot_ref, nope_ref, rope_ref, w_ref, nk_ref, q_ref, n_ref, perm_ref, own_ref):
    tiles, heads, per, wide = q_ref.shape
    rows = nope_ref.shape[2]
    nope = w_ref.shape[2]
    lat = w_ref.shape[3]
    total = tiles * per

    @pl.when(pl.program_id(0) == 0)
    def _():
        places = row_places(slot_ref)
        lane = lax.broadcasted_iota(jnp.int32, (1, steps * rows), 1)
        step_of = lane // rows
        row_of = lane - step_of * rows
        where_to = jnp.full((1, steps * rows), -1, jnp.int32)
        for r in range(rows):
            where_to = jnp.where(row_of == r, places[r], where_to)
        place, step = order_index(0, (total, steps * rows), steps)
        perm_ref[...] = jnp.where((place == where_to) & (step == step_of), 1.0, 0.0).astype(BF)
        lane1 = lax.broadcasted_iota(jnp.int32, (total, rows), 1)
        place1, _ = order_index(0, (total, rows), steps)
        where1 = jnp.full((1, rows), -1, jnp.int32)
        lane_r = lax.broadcasted_iota(jnp.int32, (1, rows), 1)
        for r in range(rows):
            where1 = jnp.where(lane_r == r, places[r], where1)
        by_row = jnp.where(place1 == where1, 1.0, 0.0).astype(BF)
        for s in range(steps):
            own_ref[s] = jnp.dot(by_row, nk_ref[s, 0], preferred_element_type=F32)

    perm = perm_ref[...]
    x = nope_ref[:, 0].reshape(steps * rows, heads * nope)
    x = jnp.dot(perm, x, preferred_element_type=F32).astype(BF)
    r = rope_ref[:, 0].reshape(steps * rows, 128)
    r = jnp.dot(perm, r, preferred_element_type=F32)
    rolled = pltpu.roll(r, 64, 1)
    lane = lax.broadcasted_iota(jnp.int32, (total, 128), 1)
    mine = (lane // 64) == layer
    _, step = order_index(0, (total, 1), steps)
    for h in range(heads):
        ql = jnp.dot(x[:, h * nope:(h + 1) * nope], w_ref[0, h], preferred_element_type=F32).astype(BF)
        qr = jnp.where(mine, r if h == layer else rolled, 0.0).astype(BF)
        q = jnp.concatenate([ql, qr], axis=1)
        q_ref[:, h] = q.reshape(tiles, per, wide)
        qf = q.astype(F32)
        scores = []
        for s in range(steps):
            v = jnp.sum(qf * own_ref[s], axis=1, keepdims=True) * scale
            scores.append(jnp.where(step >= s, v, LOW))
        top = split2(functools.reduce(jnp.maximum, scores))
        weights = [jnp.exp(v - (top[0] + top[1])) for v in scores]
        o = weights[0] * own_ref[0, :, :lat]
        for s in range(1, steps):
            o = o + weights[s] * own_ref[s, :, :lat]
        part = partial_of(o, top, split2(sum(weights)))
        n_ref[:, h] = part.astype(BF).reshape(tiles, per, wide)


def queries(layer, tiles, scale, row_slot, q_nope, q_rope, w_uk, nk):
    steps, _, rows, _ = q_nope.shape
    _, heads, nope, lat = w_uk.shape
    wide = nk.shape[3]
    per = TILE_ROWS * steps
    shape = jax.ShapeDtypeStruct((tiles, heads, per, wide), BF)
    return pl.pallas_call(
        functools.partial(query_body, layer, steps, scale),
        grid=(heads // 2,),
        in_specs=[
            pl.BlockSpec(memory_space=pltpu.SMEM),
            pl.BlockSpec((steps, 1, rows, 2 * nope), lambda h: (0, layer, 0, h)),
            pl.BlockSpec((steps, 1, rows, 128), lambda h: (0, layer, 0, h)),
            pl.BlockSpec((1, 2, nope, lat), lambda h: (layer, h, 0, 0)),
            pl.BlockSpec((steps, 1, rows, wide), lambda h: (0, layer, 0, 0)),
        ],
        out_specs=[pl.BlockSpec((tiles, 2, per, wide), lambda h: (0, h, 0, 0))] * 2,
        out_shape=[shape, shape],
        scratch_shapes=[
            pltpu.VMEM((tiles * per, steps * rows), BF),
            pltpu.VMEM((steps, tiles * per, wide), F32),
        ],
        compiler_params=params(16),
        cost_estimate=cost(2 * tiles * per * heads * nope * lat, w_uk.size + 4 * tiles * per * heads * wide),
        name="queries",
    )(row_slot, q_nope, q_rope, w_uk, nk)


def attend_body(layer, scale, shifts, slot_ref, assign_ref, len_ref, qa_hbm, qb_hbm, *refs):
    names = [(k, i) for k in shifts for i in range(2 if k == 2 else 1)]
    pieces = refs[:len(names)]
    ropes = refs[len(names):2 * len(names)] if layer else None
    oa_ref, ob_ref, keys, qa_ref, qb_ref, kept, sems, q_sems = refs[-8:]
    slots = keys.shape[0]
    group = lax.axis_index("section")
    head = lax.axis_index("head")
    y = lax.div(head, jnp.int32(2))
    core = lax.rem(head, jnp.int32(2))
    wide = keys.shape[-1]
    lat = wide - 128
    block = keys.shape[2] * keys.shape[3]
    tiles, heads, per, _ = oa_ref.shape
    count = heads * per
    half = keys.shape[2] // 2
    own = lat if layer else wide
    origin = {k: lax.rem(y - k + 4, jnp.int32(4)) for k in shifts}

    def copies(s):
        out = []
        for j, (k, i) in enumerate(names):
            at = sum(jnp.where(origin[o] < origin[k], 1, 0) for o in shifts)
            to = pl.ds(i * half, half) if k == 2 else pl.ds(0, 2 * half)
            out.append(pltpu.make_async_copy(
                pieces[j].at[:, s], keys.at[s, at, to, :, pl.ds(0, own)], sems.at[k, s, i]))
            if layer:
                out.append(pltpu.make_async_copy(
                    ropes[j].at[:, s, :, pl.ds(lat, 128)], keys.at[s, at, to, :, pl.ds(lat, 128)],
                    sems.at[k, s, 2 + i]))
        return out

    def query_copies(tile):
        return [
            pltpu.make_async_copy(held.at[tile], here.at[tile], q_sems.at[tile, i])
            for i, (held, here) in enumerate(((qa_hbm, qa_ref), (qb_hbm, qb_ref)))
        ]

    moving = [copies(s) for s in range(slots)]
    for c in moving[0] + query_copies(0) + moving[1]:
        c.start()
    for tile in range(1, tiles):
        for c in query_copies(tile):
            c.start()
    for c in moving[0] + moving[1]:
        c.wait()
    zeros = count_zeros(slot_ref)
    factor = scale * math.log2(math.e)

    def arrive(tile, slot):
        @pl.when((slot == 0) | (tile * TILE_ROWS >= zeros))
        def _():
            for c in query_copies(tile):
                c.wait()

    def put(o_ref, tile, r):
        o_ref[tile] = r.astype(BF).reshape(heads, per, wide)

    def chains(todo, slot, n, left):
        k = keys[slot, 0:n].reshape(n * block, wide)
        lane = lax.broadcasted_iota(jnp.int32, (count, block), 1)
        jobs = [(tile, q_ref, o_ref) for tile in todo for q_ref, o_ref in ((qa_ref, oa_ref), (qb_ref, ob_ref))]

        def scores_of(job):
            return lax.dot_general(
                job[1][job[0]].reshape(count, wide), k, (((1,), (1,)), ((), ())), preferred_element_type=F32)

        lead = 4 if n <= 2 else 2
        ahead = [scores_of(job) for job in jobs[:lead]]
        for i, (tile, _, o_ref) in enumerate(jobs):
            if i + lead < len(jobs):
                ahead.append(scores_of(jobs[i + lead]))
            s = ahead[i]
            last = jnp.where(lane < left, s[:, (n - 1) * block:], LOW)
            s = last if n == 1 else jnp.concatenate([s[:, :(n - 1) * block], last], axis=1)
            top = split2(jnp.max(s, axis=1, keepdims=True) * scale)
            p = jnp.exp2(s * factor - (top[0] + top[1]) * math.log2(math.e))
            total = jnp.sum(p, axis=1, keepdims=True)
            o = jnp.dot(p.astype(BF), k[:, :lat], preferred_element_type=F32)
            put(o_ref, tile, partial_of(o, top, split2(total)))

    def one_slot(slot, carry):
        begin = jnp.where(slot == 0, 0, lax.div(zeros, jnp.int32(TILE_ROWS)))
        end = jnp.where(slot == 0, lax.div(zeros + (TILE_ROWS - 1), jnp.int32(TILE_ROWS)), tiles)
        length = len_ref[assign_ref[group * slots + slot]]
        prefix = lax.div(length - block * core + (2 * block - 1), jnp.int32(2 * block))
        blocks = sum(jnp.where(origin[k] < prefix, 1, 0) for k in shifts)
        final = functools.reduce(jnp.maximum, [jnp.where(origin[k] < prefix, origin[k], 0) for k in shifts])
        left = length - (2 * final + core) * block
        pairs = lax.div(end - begin, jnp.int32(2))
        shared = (slot == 1) & (begin * TILE_ROWS < zeros)

        @pl.when(shared)
        def _():
            kept[0] = oa_ref[begin]
            kept[1] = ob_ref[begin]

        @pl.when(blocks == 0)
        def _():
            nothing = partial_of(jnp.zeros((count, lat), F32), (jnp.full((count, 1), LOW, F32),), ())

            def fill(tile, c):
                arrive(tile, slot)
                put(oa_ref, tile, nothing)
                put(ob_ref, tile, nothing)
                return c

            lax.fori_loop(begin, end, fill, 0)

        for n in range(1, len(shifts) + 1):
            @pl.when(blocks == n)
            def _(n=n):
                def pair(i, c):
                    arrive(begin + 2 * i, slot)
                    arrive(begin + 2 * i + 1, slot)
                    chains([begin + 2 * i, begin + 2 * i + 1], slot, n, left)
                    return c

                lax.fori_loop(0, pairs, pair, 0)

                @pl.when(begin + 2 * pairs < end)
                def _():
                    arrive(end - 1, slot)
                    chains([end - 1], slot, n, left)

        @pl.when(shared)
        def _():
            i = lax.broadcasted_iota(jnp.int32, (count, 1), 0)
            before = begin * TILE_ROWS + lax.rem(i, jnp.int32(TILE_ROWS)) < zeros
            for old, o_ref in enumerate((oa_ref, ob_ref)):
                a = kept[old].reshape(count, wide).astype(F32)
                b = o_ref[begin].reshape(count, wide).astype(F32)
                put(o_ref, begin, jnp.where(before, a, b))
        return carry

    lax.fori_loop(0, slots, one_slot, 0)


def attend(layer, scale, shifts, row_slot, assign, prompt_len, qa, qb, pieces, ropes):
    tiles, heads, per, wide = qa.shape
    parts, slots, rows, _ = ropes[0].shape
    smem = pl.BlockSpec(memory_space=pltpu.SMEM)
    vmem = pl.BlockSpec(memory_space=pltpu.VMEM)
    held = list(pieces) + (list(ropes) if layer else [])
    shape = jax.ShapeDtypeStruct(qa.shape, BF)
    part = len(shifts)
    parts = parts if 2 not in shifts or part > 1 else 2 * parts
    return pl.pallas_call(
        functools.partial(attend_body, layer, scale, shifts),
        in_specs=[smem] * 3 + [pl.BlockSpec(memory_space=pl.ANY)] * (2 + len(held)),
        out_specs=[vmem] * 2,
        out_shape=[shape, shape],
        scratch_shapes=[
            pltpu.VMEM((slots, part, parts, rows, wide), BF),
            pltpu.VMEM(qa.shape, BF),
            pltpu.VMEM(qa.shape, BF),
            pltpu.VMEM((2, heads, per, wide), BF),
            pltpu.SemaphoreType.DMA((4, slots, 4)),
            pltpu.SemaphoreType.DMA((tiles, 2)),
        ],
        compiler_params=params(32),
        cost_estimate=cost(2 * 2 * tiles * heads * per * part * parts * rows * 1152, 4 * qa.size * 2, 0),
        name="attend",
    )(row_slot, assign, prompt_len, qa, qb, *held)


def merge_body(layer, steps, count, slot_ref, w_ref, *refs):
    o_ref = refs[-1]
    partials = refs[:count]
    tiles, heads, per, wide = partials[0].shape
    lat = wide - 128
    total = tiles * per
    rows = o_ref.shape[2]
    value = w_ref.shape[3]

    places = row_places(slot_ref)
    sub = lax.broadcasted_iota(jnp.int32, (steps * rows, total), 0)
    step_of = sub // rows
    row_of = sub - step_of * rows
    where_to = jnp.full((steps * rows, total), -1, jnp.int32)
    for r in range(rows):
        where_to = jnp.where(row_of == r, places[r], where_to)
    place, step = order_index(1, (steps * rows, total), steps)
    back = jnp.where((place == where_to) & (step == step_of), 1.0, 0.0).astype(BF)

    lane = lax.broadcasted_iota(jnp.int32, (128, 128), 0)
    spread_top = jnp.where(lane < 2, 1.0, 0.0).astype(BF)
    spread_total = jnp.where((lane >= 2) & (lane < 4), 1.0, 0.0).astype(BF)
    every = tiles * heads * per
    tails = [r[:, :, :, lat:].reshape(every, 128) for r in partials]
    tops = [jnp.dot(v, spread_top, preferred_element_type=F32) for v in tails]
    totals = [jnp.dot(v, spread_total, preferred_element_type=F32) for v in tails]
    top = functools.reduce(jnp.maximum, tops)
    w = [jnp.exp(v - top) for v in tops]
    inv = 1.0 / sum(wi * v for wi, v in zip(w, totals))
    w = [wi * inv for wi in w]
    o = jnp.concatenate([
        sum(wi * r[:, :, :, c:c + 128].reshape(every, 128).astype(F32) for wi, r in zip(w, partials)).astype(BF)
        for c in range(0, lat, 128)
    ], axis=1).reshape(tiles, heads, per, lat)
    res = [
        jnp.dot(o[:, h].reshape(total, lat), w_ref[layer, h], preferred_element_type=F32).astype(BF)
        for h in range(heads)
    ]
    res = jnp.dot(back, jnp.concatenate(res, axis=1), preferred_element_type=F32).astype(BF)
    o_ref[:, 0] = res.reshape(steps, rows, heads * value)


def merge(layer, layers, steps, rows, row_slot, partials, w_uv, before):
    tiles, heads, per, wide = partials[0].shape
    lat, value = w_uv.shape[2:]
    vmem = pl.BlockSpec(memory_space=pltpu.VMEM)
    held = [] if before is None else [before]
    return pl.pallas_call(
        functools.partial(merge_body, layer, steps, len(partials)),
        grid=(1,),
        in_specs=[pl.BlockSpec(memory_space=pltpu.SMEM)] + [vmem] * (1 + len(partials))
        + [pl.BlockSpec(memory_space=pl.ANY)] * len(held),
        out_specs=pl.BlockSpec((steps, 1, rows, heads * value), lambda i: (0, layer, 0, 0)),
        out_shape=jax.ShapeDtypeStruct((steps, layers, rows, heads * value), BF),
        input_output_aliases={2 + len(partials): 0} if held else {},
        compiler_params=params(24),
        cost_estimate=cost(2 * tiles * per * heads * lat * value, len(partials) * partials[0].size * 2),
        name="merge",
    )(row_slot, w_uv, *partials, *held)


def local(n_section, n_head, kv_cache, prompt_len, assign, row_slot, q_nope, q_rope, new_kv, w_uk, w_uv):
    layers = kv_cache.shape[0]
    steps, _, rows, _ = q_nope.shape
    _, heads, nope, lat = w_uk.shape
    width = kv_cache.shape[3]
    rope = width - lat
    scale = (nope + rope) ** (-0.5)
    tiles = rows // TILE_ROWS
    chips = n_head // 2

    def spread(x):
        return lax.all_to_all(x, "section", 0, 0, tiled=True)

    def step_y(x, k):
        return lax.ppermute(x, "head", [(h, ((h // 2 + k) % chips) * 2 + h % 2) for h in range(n_head)])

    def onward(up, down):
        half = up.shape[0] // 2
        return [step_y(up[:half], 1), step_y(down[half:], -1)]

    def swap(x):
        return lax.ppermute(x, "head", [(h, h ^ 1) for h in range(n_head)])

    zero = jnp.zeros((steps, rows, rope), BF)
    nk = jnp.stack([
        jnp.concatenate([new_kv[:, 0], zero], axis=2),
        jnp.concatenate([new_kv[:, 1, :, :lat], zero, new_kv[:, 1, :, lat:]], axis=2),
    ], axis=1)
    qn = [queries(layer, tiles, scale, row_slot, q_nope, q_rope, w_uk, nk) for layer in range(layers)]
    sib = [swap(q) for q, _ in qn]

    x = spread(pack(kv_cache, n_section, lat))
    x, qn = lax.optimization_barrier((x, qn))
    picked = [pick(layer, lat, assign, x) for layer in range(layers)]
    k0, sib, later = lax.optimization_barrier((spread(picked[0]), sib, picked[1]))
    k1 = spread(later)
    up, down = step_y(k0, 1), step_y(k0, -1)
    up, down, k1 = lax.optimization_barrier((up, down, k1))
    near0, far0 = [k0, up, down], onward(up, down)
    up, down = step_y(k1, 1), step_y(k1, -1)
    order = (0, 1, 3, 2)

    def attended(layer, shifts, pieces, ropes):
        return attend(layer, scale, shifts, row_slot, assign, prompt_len, qn[layer][0], sib[layer], pieces, ropes)

    first = attended(0, order[:3], near0, near0)
    first, up, down = lax.optimization_barrier((first, up, down))
    p1 = [k1, up, down] + onward(up, down)
    calls = [[first, attended(0, order[3:], far0, far0)], [attended(1, order, p1, near0 + far0)]]
    out = None
    for layer in range(layers):
        partials = [x for mine, theirs in calls[layer] for x in (mine, swap(theirs))]
        out = merge(layer, layers, steps, rows, row_slot, partials + [qn[layer][1]], w_uv, out)
    return out


def solution(mesh):
    in_specs = (
        P(None, "section", "head", None),
        P(),
        P(),
        P("section"),
        P(None, None, "section", "head"),
        P(None, None, "section", "head"),
        P(None, None, "section", None),
        P(None, "head", None, None),
        P(None, "head", None, None),
    )
    out_specs = P(None, None, "section", "head")
    step = functools.partial(local, mesh.shape["section"], mesh.shape["head"])
    return jax.shard_map(step, mesh=mesh, in_specs=in_specs, out_specs=out_specs, check_vma=False)
```

```python
import functools
import math

import jax
import jax.numpy as jnp
from jax import lax
from jax.experimental import pallas as pl
from jax.experimental.pallas import tpu as pltpu
from jax.sharding import PartitionSpec as P

BF = jnp.bfloat16
F32 = jnp.float32
TILE_ROWS = 8
LOW = -1e30
MIB = 1 << 20


def params(limit, **extra):
    return pltpu.CompilerParams(vmem_limit_bytes=limit * MIB, **extra)


def cost(flops, nbytes, trans=0):
    return pl.CostEstimate(flops=int(flops), bytes_accessed=int(nbytes), transcendentals=int(trans))


def pack_body(lat, kv_ref, x_ref):
    parts, _, rows, wide = x_ref.shape
    a = kv_ref[0, 0].T
    b = kv_ref[1, 0].T
    x = jnp.concatenate([a[:, :lat], b[:, :lat], a[:, lat:], b[:, lat:]], axis=1)
    x_ref[:, 0] = x.reshape(parts, rows, wide)


def pack(kv, parts, lat):
    layers, prompts, tok, width = kv.shape
    rows = tok // parts
    return pl.pallas_call(
        functools.partial(pack_body, lat),
        grid=(prompts,),
        in_specs=[pl.BlockSpec((layers, 1, width, tok), lambda p: (0, p, 0, 0))],
        out_specs=pl.BlockSpec((parts, 1, rows, layers * width), lambda p: (0, p, 0, 0)),
        out_shape=jax.ShapeDtypeStruct((parts, prompts, rows, layers * width), BF),
        compiler_params=params(60),
        cost_estimate=cost(0, 2 * kv.size * 2),
        name="pack",
    )(kv.transpose(0, 1, 3, 2))


def pick_body(layer, lat, assign_ref, x_ref, o_ref):
    for i in range(o_ref.shape[0]):
        p = assign_ref[i]
        o_ref[i, :, :lat] = x_ref[p, :, layer * lat:(layer + 1) * lat]
        if layer == 0:
            o_ref[i, :, lat:] = x_ref[p, :, 2 * lat:]


def pick(layer, lat, assign, x):
    groups, slots, rows, wide = x.shape
    out = lat if layer else wide - lat
    res = pl.pallas_call(
        functools.partial(pick_body, layer, lat),
        in_specs=[
            pl.BlockSpec(memory_space=pltpu.SMEM),
            pl.BlockSpec(memory_space=pltpu.VMEM),
        ],
        out_specs=pl.BlockSpec(memory_space=pltpu.VMEM),
        out_shape=jax.ShapeDtypeStruct((groups * slots, rows, out), BF),
        compiler_params=params(16),
        cost_estimate=cost(0, 2 * x.size * 2),
        name="pick",
    )(assign, x.reshape(groups * slots, rows, wide))
    return res.reshape(groups, slots, rows, out)


def count_zeros(slot_ref):
    zeros = jnp.int32(slot_ref.shape[0])
    for r in range(slot_ref.shape[0]):
        zeros = zeros - slot_ref[r]
    return zeros


def row_places(slot_ref):
    places = []
    c0, c1 = jnp.int32(0), count_zeros(slot_ref)
    for r in range(slot_ref.shape[0]):
        s = slot_ref[r]
        places.append(jnp.where(s == 0, c0, c1))
        c0 = c0 + (1 - s)
        c1 = c1 + s
    return places


def order_index(axis, shape, steps):
    i = lax.broadcasted_iota(jnp.int32, shape, axis)
    per = TILE_ROWS * steps
    tile = i // per
    rest = i - tile * per
    step = rest // TILE_ROWS
    return tile * TILE_ROWS + (rest - step * TILE_ROWS), step


def split2(x):
    hi = x.astype(BF).astype(F32)
    return hi, (x - hi).astype(BF).astype(F32)


def partial_of(o, top, total):
    lane = lax.broadcasted_iota(jnp.int32, (o.shape[0], 128), 1)
    tail = jnp.zeros((o.shape[0], 128), F32)
    for i, v in enumerate(top + total):
        tail = jnp.where(lane == i, v, tail)
    return jnp.concatenate([o, tail], axis=1)


def query_body(layer, steps, scale, slot_ref, nope_ref, rope_ref, w_ref, nk_ref, q_ref, n_ref, perm_ref, own_ref):
    tiles, heads, per, wide = q_ref.shape
    rows = nope_ref.shape[2]
    nope = w_ref.shape[2]
    lat = w_ref.shape[3]
    total = tiles * per

    @pl.when(pl.program_id(0) == 0)
    def _():
        places = row_places(slot_ref)
        lane = lax.broadcasted_iota(jnp.int32, (1, steps * rows), 1)
        step_of = lane // rows
        row_of = lane - step_of * rows
        where_to = jnp.full((1, steps * rows), -1, jnp.int32)
        for r in range(rows):
            where_to = jnp.where(row_of == r, places[r], where_to)
        place, step = order_index(0, (total, steps * rows), steps)
        perm_ref[...] = jnp.where((place == where_to) & (step == step_of), 1.0, 0.0).astype(BF)
        lane1 = lax.broadcasted_iota(jnp.int32, (total, rows), 1)
        place1, _ = order_index(0, (total, rows), steps)
        where1 = jnp.full((1, rows), -1, jnp.int32)
        lane_r = lax.broadcasted_iota(jnp.int32, (1, rows), 1)
        for r in range(rows):
            where1 = jnp.where(lane_r == r, places[r], where1)
        by_row = jnp.where(place1 == where1, 1.0, 0.0).astype(BF)
        for s in range(steps):
            own_ref[s] = jnp.dot(by_row, nk_ref[s, 0], preferred_element_type=F32)

    perm = perm_ref[...]
    x = nope_ref[:, 0].reshape(steps * rows, heads * nope)
    x = jnp.dot(perm, x, preferred_element_type=F32).astype(BF)
    r = rope_ref[:, 0].reshape(steps * rows, 128)
    r = jnp.dot(perm, r, preferred_element_type=F32)
    rolled = pltpu.roll(r, 64, 1)
    lane = lax.broadcasted_iota(jnp.int32, (total, 128), 1)
    mine = (lane // 64) == layer
    _, step = order_index(0, (total, 1), steps)
    for h in range(heads):
        ql = jnp.dot(x[:, h * nope:(h + 1) * nope], w_ref[0, h], preferred_element_type=F32).astype(BF)
        qr = jnp.where(mine, r if h == layer else rolled, 0.0).astype(BF)
        q = jnp.concatenate([ql, qr], axis=1)
        q_ref[:, h] = q.reshape(tiles, per, wide)
        qf = q.astype(F32)
        scores = []
        for s in range(steps):
            v = jnp.sum(qf * own_ref[s], axis=1, keepdims=True) * scale
            scores.append(jnp.where(step >= s, v, LOW))
        top = split2(functools.reduce(jnp.maximum, scores))
        weights = [jnp.exp(v - (top[0] + top[1])) for v in scores]
        o = weights[0] * own_ref[0, :, :lat]
        for s in range(1, steps):
            o = o + weights[s] * own_ref[s, :, :lat]
        part = partial_of(o, top, split2(sum(weights)))
        n_ref[:, h] = part.astype(BF).reshape(tiles, per, wide)


def queries(layer, tiles, scale, row_slot, q_nope, q_rope, w_uk, nk):
    steps, _, rows, _ = q_nope.shape
    _, heads, nope, lat = w_uk.shape
    wide = nk.shape[3]
    per = TILE_ROWS * steps
    shape = jax.ShapeDtypeStruct((tiles, heads, per, wide), BF)
    return pl.pallas_call(
        functools.partial(query_body, layer, steps, scale),
        grid=(heads // 2,),
        in_specs=[
            pl.BlockSpec(memory_space=pltpu.SMEM),
            pl.BlockSpec((steps, 1, rows, 2 * nope), lambda h: (0, layer, 0, h)),
            pl.BlockSpec((steps, 1, rows, 128), lambda h: (0, layer, 0, h)),
            pl.BlockSpec((1, 2, nope, lat), lambda h: (layer, h, 0, 0)),
            pl.BlockSpec((steps, 1, rows, wide), lambda h: (0, layer, 0, 0)),
        ],
        out_specs=[pl.BlockSpec((tiles, 2, per, wide), lambda h: (0, h, 0, 0))] * 2,
        out_shape=[shape, shape],
        scratch_shapes=[
            pltpu.VMEM((tiles * per, steps * rows), BF),
            pltpu.VMEM((steps, tiles * per, wide), F32),
        ],
        compiler_params=params(16),
        cost_estimate=cost(2 * tiles * per * heads * nope * lat, w_uk.size + 4 * tiles * per * heads * wide),
        name="queries",
    )(row_slot, q_nope, q_rope, w_uk, nk)


def attend_body(layer, scale, shifts, slot_ref, assign_ref, len_ref, qa_hbm, qb_hbm, *refs):
    names = [(k, i) for k in shifts for i in range(2 if k == 2 else 1)]
    pieces = refs[:len(names)]
    ropes = refs[len(names):2 * len(names)] if layer else None
    oa_ref, ob_ref, keys, qa_ref, qb_ref, kept, sems, q_sems = refs[-8:]
    slots = keys.shape[0]
    group = lax.axis_index("section")
    head = lax.axis_index("head")
    y = lax.div(head, jnp.int32(2))
    core = lax.rem(head, jnp.int32(2))
    wide = keys.shape[-1]
    lat = wide - 128
    block = keys.shape[2] * keys.shape[3]
    tiles, heads, per, _ = oa_ref.shape
    count = heads * per
    half = keys.shape[2] // 2
    own = lat if layer else wide
    origin = {k: lax.rem(y - k + 4, jnp.int32(4)) for k in shifts}

    def copies(s):
        out = []
        for j, (k, i) in enumerate(names):
            at = sum(jnp.where(origin[o] < origin[k], 1, 0) for o in shifts)
            to = pl.ds(i * half, half) if k == 2 else pl.ds(0, 2 * half)
            out.append(pltpu.make_async_copy(
                pieces[j].at[:, s], keys.at[s, at, to, :, pl.ds(0, own)], sems.at[k, s, i]))
            if layer:
                out.append(pltpu.make_async_copy(
                    ropes[j].at[:, s, :, pl.ds(lat, 128)], keys.at[s, at, to, :, pl.ds(lat, 128)],
                    sems.at[k, s, 2 + i]))
        return out

    def query_copies(tile):
        return [
            pltpu.make_async_copy(held.at[tile], here.at[tile], q_sems.at[tile, i])
            for i, (held, here) in enumerate(((qa_hbm, qa_ref), (qb_hbm, qb_ref)))
        ]

    moving = [copies(s) for s in range(slots)]
    for c in moving[0] + query_copies(0) + moving[1]:
        c.start()
    for tile in range(1, tiles):
        for c in query_copies(tile):
            c.start()
    for c in moving[0] + moving[1]:
        c.wait()
    zeros = count_zeros(slot_ref)
    factor = scale * math.log2(math.e)

    def arrive(tile, slot):
        @pl.when((slot == 0) | (tile * TILE_ROWS >= zeros))
        def _():
            for c in query_copies(tile):
                c.wait()

    def put(o_ref, tile, r):
        o_ref[tile] = r.astype(BF).reshape(heads, per, wide)

    def chains(todo, slot, n, left):
        k = keys[slot, 0:n].reshape(n * block, wide)
        lane = lax.broadcasted_iota(jnp.int32, (count, block), 1)
        jobs = [(tile, q_ref, o_ref) for tile in todo for q_ref, o_ref in ((qa_ref, oa_ref), (qb_ref, ob_ref))]

        def scores_of(job):
            return lax.dot_general(
                job[1][job[0]].reshape(count, wide), k, (((1,), (1,)), ((), ())), preferred_element_type=F32)

        lead = 4 if n <= 2 else 2
        ahead = [scores_of(job) for job in jobs[:lead]]
        for i, (tile, _, o_ref) in enumerate(jobs):
            if i + lead < len(jobs):
                ahead.append(scores_of(jobs[i + lead]))
            s = ahead[i]
            last = jnp.where(lane < left, s[:, (n - 1) * block:], LOW)
            s = last if n == 1 else jnp.concatenate([s[:, :(n - 1) * block], last], axis=1)
            top = split2(jnp.max(s, axis=1, keepdims=True) * scale)
            p = jnp.exp2(s * factor - (top[0] + top[1]) * math.log2(math.e))
            total = jnp.sum(p, axis=1, keepdims=True)
            o = jnp.dot(p.astype(BF), k[:, :lat], preferred_element_type=F32)
            put(o_ref, tile, partial_of(o, top, split2(total)))

    def one_slot(slot, carry):
        begin = jnp.where(slot == 0, 0, lax.div(zeros, jnp.int32(TILE_ROWS)))
        end = jnp.where(slot == 0, lax.div(zeros + (TILE_ROWS - 1), jnp.int32(TILE_ROWS)), tiles)
        length = len_ref[assign_ref[group * slots + slot]]
        prefix = lax.div(length - block * core + (2 * block - 1), jnp.int32(2 * block))
        blocks = sum(jnp.where(origin[k] < prefix, 1, 0) for k in shifts)
        final = functools.reduce(jnp.maximum, [jnp.where(origin[k] < prefix, origin[k], 0) for k in shifts])
        left = length - (2 * final + core) * block
        pairs = lax.div(end - begin, jnp.int32(2))
        shared = (slot == 1) & (begin * TILE_ROWS < zeros)

        @pl.when(shared)
        def _():
            kept[0] = oa_ref[begin]
            kept[1] = ob_ref[begin]

        @pl.when(blocks == 0)
        def _():
            nothing = partial_of(jnp.zeros((count, lat), F32), (jnp.full((count, 1), LOW, F32),), ())

            def fill(tile, c):
                arrive(tile, slot)
                put(oa_ref, tile, nothing)
                put(ob_ref, tile, nothing)
                return c

            lax.fori_loop(begin, end, fill, 0)

        for n in range(1, len(shifts) + 1):
            @pl.when(blocks == n)
            def _(n=n):
                def pair(i, c):
                    arrive(begin + 2 * i, slot)
                    arrive(begin + 2 * i + 1, slot)
                    chains([begin + 2 * i, begin + 2 * i + 1], slot, n, left)
                    return c

                lax.fori_loop(0, pairs, pair, 0)

                @pl.when(begin + 2 * pairs < end)
                def _():
                    arrive(end - 1, slot)
                    chains([end - 1], slot, n, left)

        @pl.when(shared)
        def _():
            i = lax.broadcasted_iota(jnp.int32, (count, 1), 0)
            before = begin * TILE_ROWS + lax.rem(i, jnp.int32(TILE_ROWS)) < zeros
            for old, o_ref in enumerate((oa_ref, ob_ref)):
                a = kept[old].reshape(count, wide).astype(F32)
                b = o_ref[begin].reshape(count, wide).astype(F32)
                put(o_ref, begin, jnp.where(before, a, b))
        return carry

    lax.fori_loop(0, slots, one_slot, 0)


def attend(layer, scale, shifts, row_slot, assign, prompt_len, qa, qb, pieces, ropes):
    tiles, heads, per, wide = qa.shape
    parts, slots, rows, _ = ropes[0].shape
    smem = pl.BlockSpec(memory_space=pltpu.SMEM)
    vmem = pl.BlockSpec(memory_space=pltpu.VMEM)
    held = list(pieces) + (list(ropes) if layer else [])
    shape = jax.ShapeDtypeStruct(qa.shape, BF)
    part = len(shifts)
    parts = parts if 2 not in shifts or part > 1 else 2 * parts
    return pl.pallas_call(
        functools.partial(attend_body, layer, scale, shifts),
        in_specs=[smem] * 3 + [pl.BlockSpec(memory_space=pl.ANY)] * (2 + len(held)),
        out_specs=[vmem] * 2,
        out_shape=[shape, shape],
        scratch_shapes=[
            pltpu.VMEM((slots, part, parts, rows, wide), BF),
            pltpu.VMEM(qa.shape, BF),
            pltpu.VMEM(qa.shape, BF),
            pltpu.VMEM((2, heads, per, wide), BF),
            pltpu.SemaphoreType.DMA((4, slots, 4)),
            pltpu.SemaphoreType.DMA((tiles, 2)),
        ],
        compiler_params=params(32),
        cost_estimate=cost(2 * 2 * tiles * heads * per * part * parts * rows * 1152, 4 * qa.size * 2, 0),
        name="attend",
    )(row_slot, assign, prompt_len, qa, qb, *held)


def merge_body(layer, steps, count, slot_ref, w_ref, *refs):
    o_ref = refs[-1]
    partials = refs[:count]
    tiles, heads, per, wide = partials[0].shape
    lat = wide - 128
    total = tiles * per
    rows = o_ref.shape[2]
    value = w_ref.shape[3]

    places = row_places(slot_ref)
    sub = lax.broadcasted_iota(jnp.int32, (steps * rows, total), 0)
    step_of = sub // rows
    row_of = sub - step_of * rows
    where_to = jnp.full((steps * rows, total), -1, jnp.int32)
    for r in range(rows):
        where_to = jnp.where(row_of == r, places[r], where_to)
    place, step = order_index(1, (steps * rows, total), steps)
    back = jnp.where((place == where_to) & (step == step_of), 1.0, 0.0).astype(BF)

    lane = lax.broadcasted_iota(jnp.int32, (128, 128), 0)
    spread_top = jnp.where(lane < 2, 1.0, 0.0).astype(BF)
    spread_total = jnp.where((lane >= 2) & (lane < 4), 1.0, 0.0).astype(BF)
    every = tiles * heads * per
    tails = [r[:, :, :, lat:].reshape(every, 128) for r in partials]
    tops = [jnp.dot(v, spread_top, preferred_element_type=F32) for v in tails]
    totals = [jnp.dot(v, spread_total, preferred_element_type=F32) for v in tails]
    top = functools.reduce(jnp.maximum, tops)
    w = [jnp.exp(v - top) for v in tops]
    inv = 1.0 / sum(wi * v for wi, v in zip(w, totals))
    w = [wi * inv for wi in w]
    o = jnp.concatenate([
        sum(wi * r[:, :, :, c:c + 128].reshape(every, 128).astype(F32) for wi, r in zip(w, partials)).astype(BF)
        for c in range(0, lat, 128)
    ], axis=1).reshape(tiles, heads, per, lat)
    res = [
        jnp.dot(o[:, h].reshape(total, lat), w_ref[layer, h], preferred_element_type=F32).astype(BF)
        for h in range(heads)
    ]
    res = jnp.dot(back, jnp.concatenate(res, axis=1), preferred_element_type=F32).astype(BF)
    o_ref[:, 0] = res.reshape(steps, rows, heads * value)


def merge(layer, layers, steps, rows, row_slot, partials, w_uv, before):
    tiles, heads, per, wide = partials[0].shape
    lat, value = w_uv.shape[2:]
    vmem = pl.BlockSpec(memory_space=pltpu.VMEM)
    held = [] if before is None else [before]
    return pl.pallas_call(
        functools.partial(merge_body, layer, steps, len(partials)),
        grid=(1,),
        in_specs=[pl.BlockSpec(memory_space=pltpu.SMEM)] + [vmem] * (1 + len(partials))
        + [pl.BlockSpec(memory_space=pl.ANY)] * len(held),
        out_specs=pl.BlockSpec((steps, 1, rows, heads * value), lambda i: (0, layer, 0, 0)),
        out_shape=jax.ShapeDtypeStruct((steps, layers, rows, heads * value), BF),
        input_output_aliases={2 + len(partials): 0} if held else {},
        compiler_params=params(24),
        cost_estimate=cost(2 * tiles * per * heads * lat * value, len(partials) * partials[0].size * 2),
        name="merge",
    )(row_slot, w_uv, *partials, *held)


def local(n_section, n_head, kv_cache, prompt_len, assign, row_slot, q_nope, q_rope, new_kv, w_uk, w_uv):
    layers = kv_cache.shape[0]
    steps, _, rows, _ = q_nope.shape
    _, heads, nope, lat = w_uk.shape
    width = kv_cache.shape[3]
    rope = width - lat
    scale = (nope + rope) ** (-0.5)
    tiles = rows // TILE_ROWS
    chips = n_head // 2

    def spread(x):
        return lax.all_to_all(x, "section", 0, 0, tiled=True)

    def step_y(x, k):
        return lax.ppermute(x, "head", [(h, ((h // 2 + k) % chips) * 2 + h % 2) for h in range(n_head)])

    def onward(up, down):
        half = up.shape[0] // 2
        return [step_y(up[:half], 1), step_y(down[half:], -1)]

    def swap(x):
        return lax.ppermute(x, "head", [(h, h ^ 1) for h in range(n_head)])

    zero = jnp.zeros((steps, rows, rope), BF)
    nk = jnp.stack([
        jnp.concatenate([new_kv[:, 0], zero], axis=2),
        jnp.concatenate([new_kv[:, 1, :, :lat], zero, new_kv[:, 1, :, lat:]], axis=2),
    ], axis=1)
    qn = [queries(layer, tiles, scale, row_slot, q_nope, q_rope, w_uk, nk) for layer in range(layers)]
    sib = [swap(q) for q, _ in qn]

    x = spread(pack(kv_cache, n_section, lat))
    x, qn = lax.optimization_barrier((x, qn))
    picked = [pick(layer, lat, assign, x) for layer in range(layers)]
    k0, sib, later = lax.optimization_barrier((spread(picked[0]), sib, picked[1]))
    k1 = spread(later)
    up, down = step_y(k0, 1), step_y(k0, -1)
    up, down, k1 = lax.optimization_barrier((up, down, k1))
    near0, kept = [k0, up, down], (up, down)
    up, down = step_y(k1, 1), step_y(k1, -1)
    order = (0, 1, 3, 2)

    def attended(layer, shifts, pieces, ropes):
        return attend(layer, scale, shifts, row_slot, assign, prompt_len, qn[layer][0], sib[layer], pieces, ropes)

    first = attended(0, order[:3], near0, near0)
    first, kept = lax.optimization_barrier((first, kept))
    far0 = onward(*kept)
    first, up, down = lax.optimization_barrier((first, up, down))
    p1 = [k1, up, down] + onward(up, down)
    calls = [[first, attended(0, order[3:], far0, far0)], [attended(1, order, p1, near0 + far0)]]
    out = None
    for layer in range(layers):
        partials = [x for mine, theirs in calls[layer] for x in (mine, swap(theirs))]
        out = merge(layer, layers, steps, rows, row_slot, partials + [qn[layer][1]], w_uv, out)
    return out


def solution(mesh):
    in_specs = (
        P(None, "section", "head", None),
        P(),
        P(),
        P("section"),
        P(None, None, "section", "head"),
        P(None, None, "section", "head"),
        P(None, None, "section", None),
        P(None, "head", None, None),
        P(None, "head", None, None),
    )
    out_specs = P(None, None, "section", "head")
    step = functools.partial(local, mesh.shape["section"], mesh.shape["head"])
    return jax.shard_map(step, mesh=mesh, in_specs=in_specs, out_specs=out_specs, check_vma=False)
```
